128 devices in a mesh: row: 8 (over z, y_hi), col: 16 (over y_lo, x, core).
Axes of the slice: x: 4, y: 4 (y_hi: 2, y_lo: 2; y = y_hi * 2 + y_lo), z: 4, core: 2. Of those that a mesh axis runs over, the one named last changes fastest.
Arguments:
- traces: bfloat16 [8192, 4, 15000], P('col', None, 'row'), may hold values from -8 to 8
- file_lengths: int32 [16], replicated, may hold values from 1 to 512, 4096 in all
- gap_starts: int32 [16], replicated, may hold values from 0 to 4095
- gap_lengths: int32 [16], replicated, may hold values from 1 to 33
Outputs:
- cross: bfloat16 [32, 2, 4096, 4096], P(None, None, 'row', 'col')
The draws below stay inside these ranges and needn't reach their ends.
Inputs may be any that keep to these rules, and one draw needn't show every extreme that they name: `file_lengths`: the counts sum to 4096.
All inputs are finite; a program needn't handle non-finite values.
Results may differ from the reference program's by a relative error of at most 0.0071.
Values may be sent and summed in bfloat16 or wider, within the bound.
A program may use at most 128 MiB of HBM per device.

```python
import math
import jax
import jax.numpy as jnp
import numpy as np
from jax import lax

SAMPLES = 15000
BINS = 32
WINDOWS = 4
BLOCK = 256
GAPS = 16
CHANNELS = 4096
FILE_MOST = 512
N_COL = 16


def draw_traces(key, part):
    key = jax.random.fold_in(key, 11)
    gain_key, noise_key = jax.random.split(key)
    slot_rows = N_COL * FILE_MOST
    gain = jnp.exp(jax.random.uniform(gain_key, (slot_rows, 1, 1), jnp.float32, math.log(0.1), math.log(2.0)))
    noise = jnp.clip(jax.random.normal(noise_key, (slot_rows, WINDOWS, SAMPLES), jnp.float32), -4.0, 4.0)
    return (gain * noise).astype(jnp.bfloat16)


def place_ends(array, stream_key, low, high):
    spot = [jax.random.randint(jax.random.fold_in(stream_key, axis), (), 0, length) for axis, length in enumerate(array.shape)]
    longest = array.shape.index(max(array.shape))
    next_to = spot[:longest] + [(spot[longest] + 1) % array.shape[longest]] + spot[longest + 1:]
    return array.at[tuple(spot)].set(low).at[tuple(next_to)].set(high)


def split_up(amount, total, limit, skew):
    portions = [(1 << 20) // math.isqrt(grade ** skew) + 1 for grade in range(2, amount + 1)]
    rest, counts = total - limit - (amount - 1), [1] * (amount - 1)
    while rest > 0:
        free = [i for i in range(amount - 1) if counts[i] < limit]
        mass, left = sum([portions[i] for i in free]), rest
        for i in free:
            addition = min(limit - counts[i], max(1, left * portions[i] // mass), rest)
            counts[i] = counts[i] + addition
            rest = rest - addition
    return np.array([limit] + counts)


def uneven_parts(own_key, amount, total, most, skew):
    if amount == 2:
        one = jax.random.randint(own_key, (), max(1, total - most), min(most, total - 1) + 1)
        return jnp.stack([one, total - one])
    tallies = jnp.asarray(split_up(amount, total, most, skew), jnp.int32)
    pairs = (amount - 1) // 2
    source_of, taker = tallies[1:1 + 2 * pairs:2], tallies[2:2 + 2 * pairs:2]
    room = jnp.minimum(source_of - 1, most - taker)
    shifted = jax.random.randint(jax.random.fold_in(own_key, 1), (pairs,), 0, 1 << 20) % (room + 1)
    tallies = tallies.at[1:1 + 2 * pairs:2].set(source_of - shifted).at[2:2 + 2 * pairs:2].set(taker + shifted)
    return tallies[jax.random.permutation(jax.random.fold_in(own_key, 2), amount)]


def setup_inputs(seed: int = 0) -> dict:
    keys = jax.random.split(jax.random.key(seed), 5)
    traces = draw_traces(jax.random.fold_in(keys[4], 71), 0)
    file_lengths = uneven_parts(keys[1], N_COL, CHANNELS, FILE_MOST, 2).astype(jnp.int32)
    gap_starts = place_ends(jax.random.randint(keys[2], (GAPS,), 0, CHANNELS), jax.random.fold_in(keys[2], 1), 0, CHANNELS - 1).astype(jnp.int32)
    gap_lengths = place_ends(jax.random.randint(keys[3], (GAPS,), 1, BLOCK // 8 + 2), jax.random.fold_in(keys[3], 1), 1, (BLOCK // 8 + 2) - 1).astype(jnp.int32)
    return dict(traces=traces, file_lengths=file_lengths, gap_starts=gap_starts, gap_lengths=gap_lengths)


lowest_bin = 60
bin_stride = 15
floor_level = 0.2
half_window = 2

def dft_table(first_sample, sample_count, bin_count, window_length):
    sample = first_sample + lax.iota(jnp.int32, sample_count)
    wave = lowest_bin + bin_stride * lax.iota(jnp.int32, bin_count)
    phase = sample[:, None] * wave[None, :] % window_length
    angle = phase.astype(jnp.float32) * (2.0 * math.pi / window_length)
    taper = 0.5 - 0.5 * jnp.cos(sample.astype(jnp.float32) * (2.0 * math.pi / window_length))
    weight = taper / math.sqrt(window_length)
    table = jnp.concatenate([weight[:, None] * jnp.cos(angle), -weight[:, None] * jnp.sin(angle)], axis=1)
    return table.astype(jnp.bfloat16)

def alive(channel, gap_starts, gap_lengths):
    inside = (channel[:, None] >= gap_starts[None, :]) & (channel[:, None] < gap_starts[None, :] + gap_lengths[None, :])
    return jnp.where(jnp.any(inside, axis=1), 0.0, 1.0).astype(jnp.float32)

def whiten(spectra, live, bin_count):
    row_count = spectra.shape[0]
    parts = spectra.reshape(row_count, -1, 2, bin_count)
    magnitude = jnp.sqrt(parts[:, :, 0] * parts[:, :, 0] + parts[:, :, 1] * parts[:, :, 1])
    padded = jnp.pad(magnitude, ((0, 0), (0, 0), (half_window, half_window)))
    filled = jnp.pad(jnp.ones((bin_count,), jnp.float32), (half_window, half_window))
    running = padded[:, :, 0:bin_count]
    counted = filled[0:bin_count]
    for offset in range(1, 2 * half_window + 1):
        running = running + padded[:, :, offset:offset + bin_count]
        counted = counted + filled[offset:offset + bin_count]
    level = running / counted
    factor = live[:, None, None] / jnp.maximum(level, floor_level)
    return (parts * factor[:, :, None, :]).reshape(row_count, -1).astype(jnp.bfloat16)

def reference(traces, file_lengths, gap_starts, gap_lengths):
    channels = CHANNELS
    table = dft_table(0, SAMPLES, BINS, SAMPLES)
    flat = traces.reshape(N_COL * FILE_MOST * WINDOWS, SAMPLES)
    spectra = jnp.dot(flat, table, preferred_element_type=jnp.float32).reshape(N_COL * FILE_MOST, WINDOWS * 2 * BINS)
    ends = jnp.cumsum(file_lengths).astype(jnp.int32)
    starts = (ends - file_lengths).astype(jnp.int32)
    channel = lax.iota(jnp.int32, channels)
    owner = lax.optimization_barrier(jnp.sum((ends[None, :] <= channel[:, None]).astype(jnp.int32), axis=1)).astype(jnp.int32)
    first_of = jnp.take(starts, owner)
    source = (owner * FILE_MOST + channel - first_of).astype(jnp.int32)
    ordered = jnp.take(spectra, source, axis=0)
    whitened = whiten(ordered, alive(channel, gap_starts, gap_lengths), BINS)
    parts = whitened.reshape(channels, WINDOWS, 2, BINS)

    def one_bin(index):
        picked = lax.dynamic_index_in_dim(parts, index, axis=3, keepdims=False)
        straight = picked.reshape(channels, 2 * WINDOWS)
        rotated = jnp.stack([-picked[:, :, 1], picked[:, :, 0]], axis=2).reshape(channels, 2 * WINDOWS)
        real_part = jnp.dot(straight, straight.T, preferred_element_type=jnp.float32)
        imag_part = jnp.dot(straight, rotated.T, preferred_element_type=jnp.float32)
        return (jnp.stack([real_part, imag_part]) / WINDOWS).astype(jnp.bfloat16)
    return lax.map(one_bin, jnp.arange(BINS, dtype=jnp.int32))
```

```python
import math

import jax
import jax.numpy as jnp
import ml_dtypes
import numpy as np
from jax import lax
from jax.experimental import pallas as pl
from jax.experimental.pallas import tpu as pltpu
from jax.sharding import PartitionSpec as P

SAMPLES = 15000
BINS = 32
WINDOWS = 4
FILE_MOST = 512
N_COL = 16
N_ROW = 8
GAPS = 16
FEATURES = WINDOWS * 2 * BINS
LANES = 128
SLICE = SAMPLES // N_ROW
CHUNKS = 15
CHUNK = SLICE // CHUNKS
AHEAD = 8

lowest_bin = 60
bin_stride = 15
floor_level = 0.2
half_window = 2

VMEM_LIMIT = 60 << 20
MESH = pl.DeviceIdType.MESH


def dft_table():
    sample = np.arange(SAMPLES)
    wave = lowest_bin + bin_stride * np.arange(BINS)
    angle = (sample[:, None] * wave[None, :] % SAMPLES) * (2.0 * math.pi / SAMPLES)
    taper = 0.5 - 0.5 * np.cos(sample * (2.0 * math.pi / SAMPLES))
    weight = taper / math.sqrt(SAMPLES)
    table = np.concatenate([weight[:, None] * np.cos(angle), -weight[:, None] * np.sin(angle)], axis=1)
    table = table.astype(np.float32).astype(ml_dtypes.bfloat16)
    table = table.reshape(N_ROW, CHUNKS, CHUNK, 2 * BINS).transpose(0, 1, 3, 2)
    return np.repeat(table, WINDOWS, axis=3)


def file_bounds(lengths_ref):
    firsts, total = [], 0
    for f in range(N_COL):
        firsts.append(total)
        total = total + lengths_ref[f]
    return firsts + [total]


def dft_kernel(lengths_ref, x_hbm, table_hbm, out_ref, xs, ts, x_sem, t_sem):
    row, col = lax.axis_index("row"), lax.axis_index("col")

    def copies(c):
        return (
            pltpu.make_async_copy(table_hbm.at[row, c], ts.at[c], t_sem.at[c]),
            pltpu.make_async_copy(x_hbm.at[pl.ds(c * CHUNK, CHUNK)], xs.at[c], x_sem.at[c]),
        )

    for c in range(AHEAD):
        for copy in copies(c):
            copy.start()
    first = 0
    for f in range(N_COL):
        first = first + jnp.where(f < col, lengths_ref[f], 0)
    total = None
    for c in range(CHUNKS):
        for copy in copies(c):
            copy.wait()
        if c + AHEAD < CHUNKS:
            for copy in copies(c + AHEAD):
                copy.start()
        table = ts[c]
        window = lax.broadcasted_iota(jnp.int32, table.shape, 1) % WINDOWS
        wide = jnp.concatenate(
            [jnp.where(window == w, table, jnp.zeros_like(table)) for w in range(WINDOWS)], axis=0
        )
        samples = xs[c].reshape(CHUNK * WINDOWS, FILE_MOST)
        part = jnp.dot(wide, samples, preferred_element_type=jnp.float32)
        total = part if total is None else total + part
    turned = pltpu.roll(total, lax.rem(first, FILE_MOST), axis=1)
    for z in range(4):
        for half in range(2):
            out_ref[2 * z + half] = turned[128 * half : 128 * half + 128, LANES * z : LANES * z + LANES]


def whiten(total):
    out = []
    bins = lax.broadcasted_iota(jnp.int32, (BINS, LANES), 0)
    low = jnp.minimum(bins, half_window)
    high = jnp.minimum(BINS - 1 - bins, half_window)
    counted = (low + high + 1).astype(jnp.float32)
    edge = jnp.zeros((8, LANES), jnp.float32)
    for w in range(2):
        re = total[64 * w : 64 * w + BINS]
        im = total[64 * w + BINS : 64 * w + 2 * BINS]
        magnitude = jnp.sqrt(re * re + im * im)
        padded = jnp.concatenate([edge, magnitude, edge], axis=0)
        running = padded[8 - half_window : 8 - half_window + BINS]
        for offset in range(1 - half_window, half_window + 1):
            running = running + padded[8 + offset : 8 + offset + BINS]
        level = running / counted
        factor = 1.0 / jnp.maximum(level, floor_level)
        out.append(jnp.concatenate([re * factor, im * factor], axis=0).astype(jnp.bfloat16))
    return out


def exchange_kernel(
    lengths_ref, gap_starts_ref, gap_lengths_ref, part_ref, left_ref, right_ref,
    sums, white, files, block, rows, cols, send1, recv1, send2, recv2, send3, recv3, send4, recv4, local_sem,
):
    row, col = lax.axis_index("row"), lax.axis_index("col")
    z = row // 2
    half = row % 2
    side = col % 2
    k = col // 2
    barrier = pltpu.get_barrier_semaphore()
    for d in range(1, N_ROW):
        pl.semaphore_signal(barrier, inc=1, device_id=((row + d) % N_ROW, col), device_id_type=MESH)
    for d in range(1, N_COL):
        pl.semaphore_signal(barrier, inc=1, device_id=(row, (col + d) % N_COL), device_id_type=MESH)
    pl.semaphore_wait(barrier, N_ROW + N_COL - 2)

    def copy1(d):
        there = (row + d) % N_ROW
        return pltpu.make_async_remote_copy(
            src_ref=part_ref.at[there], dst_ref=sums.at[d - 1],
            send_sem=send1.at[d - 1], recv_sem=recv1.at[d - 1],
            device_id=(there, col), device_id_type=MESH,
        )

    for d in range(1, N_ROW):
        copy1(d).start()
    channel = FILE_MOST * k + LANES * z + lax.broadcasted_iota(jnp.int32, (1, LANES), 1)
    dead = jnp.zeros((1, LANES), jnp.bool_)
    for g in range(GAPS):
        first = gap_starts_ref[g]
        dead = dead | ((channel >= first) & (channel < first + gap_lengths_ref[g]))
    bounds = file_bounds(lengths_ref)
    total = part_ref[row]
    for d in range(1, N_ROW):
        copy1(d).wait_recv()
        total = total + sums[d - 1]
    pair = whiten(total)
    white[0] = pair[0]
    white[1] = pair[1]

    def copy2(d):
        there = (col + d) % N_COL
        return pltpu.make_async_remote_copy(
            src_ref=white.at[there % 2], dst_ref=files.at[col],
            send_sem=send2.at[d - 1], recv_sem=recv2.at[d - 1],
            device_id=(row, there), device_id_type=MESH,
        )

    for d in range(1, N_COL):
        copy2(d).start()
    files[col] = white[side]
    for d in range(1, N_COL):
        copy2(d).wait_recv()
    chosen = jnp.zeros((64, LANES), jnp.float32)
    for f in range(N_COL):
        mine = (channel >= bounds[f]) & (channel < bounds[f + 1]) & jnp.logical_not(dead)
        chosen = jnp.where(mine, files[f].astype(jnp.float32), chosen)
    block[...] = chosen.astype(jnp.bfloat16)

    at = pl.multiple_of((2 * half + side) * 64, 64)
    lane_block = z % 2
    near = 2 * k + z // 2

    def copy3(d):
        there = (col + d) % N_COL
        return pltpu.make_async_remote_copy(
            src_ref=block, dst_ref=rows.at[z, pl.ds(at, 64)],
            send_sem=send3.at[d], recv_sem=recv3.at[row * 2 + side],
            device_id=(k, there), device_id_type=MESH,
        )

    def copy4(d):
        there = (row + d) % N_ROW
        return pltpu.make_async_remote_copy(
            src_ref=block, dst_ref=cols.at[lane_block, pl.ds(at, 64)],
            send_sem=send4.at[d], recv_sem=recv4.at[lane_block * 4 + half * 2 + side],
            device_id=(there, near), device_id_type=MESH,
        )

    for d in range(1, N_COL):
        copy3(d).start()
    for d in range(1, N_ROW):
        copy4(d).start()

    @pl.when(row != k)
    def _():
        copy3(0).start()

    @pl.when(row == k)
    def _():
        rows[z, pl.ds(at, 64)] = block[...]

    @pl.when(near != col)
    def _():
        copy4(0).start()

    @pl.when(near == col)
    def _():
        cols[lane_block, pl.ds(at, 64)] = block[...]

    for d in range(1, N_ROW):
        copy1(d).wait_send()
    for d in range(1, N_COL):
        copy2(d).wait_send()
        copy3(d).wait_send()
    for d in range(1, N_ROW):
        copy4(d).wait_send()

    @pl.when(row != k)
    def _():
        copy3(0).wait_send()

    @pl.when(near != col)
    def _():
        copy4(0).wait_send()

    for source_row in range(N_ROW):
        for s in range(2):
            @pl.when(jnp.logical_or(row != source_row, col != 2 * row + s))
            def _():
                pltpu.make_async_copy(block, rows.at[0, pl.ds(0, 64)], recv3.at[source_row * 2 + s]).wait()
    for q in range(2):
        for h in range(2):
            for s in range(2):
                @pl.when(jnp.logical_or(row != 2 * (2 * side + q) + h, side != s))
                def _():
                    pltpu.make_async_copy(block, cols.at[0, pl.ds(0, 64)], recv4.at[q * 4 + h * 2 + s]).wait()
    left_ref[...] = rows[...]
    right_ref[...] = cols[...]


def cross_kernel(left_ref, right_ref, out_hbm, left, right, buffer, sem):
    for z in range(4):
        left[LANES * z : LANES * z + LANES, :] = left_ref[z].astype(jnp.float32).T.astype(jnp.bfloat16)
    for q in range(2):
        part = right_ref[q] * jnp.asarray(1.0 / WINDOWS, jnp.bfloat16)
        right[0, :, LANES * q : LANES * q + LANES] = part
        for w in range(WINDOWS):
            re = part[64 * w : 64 * w + BINS]
            im = part[64 * w + BINS : 64 * w + 2 * BINS]
            right[1, 64 * w : 64 * w + BINS, LANES * q : LANES * q + LANES] = -im
            right[1, 64 * w + BINS : 64 * w + 2 * BINS, LANES * q : LANES * q + LANES] = re
    bin_of = lax.broadcasted_iota(jnp.int32, (FEATURES, 2 * LANES), 0) % BINS

    def copy(b):
        return pltpu.make_async_copy(buffer.at[b], out_hbm.at[b], sem.at[b])

    def one_bin(b, carry):
        for q in range(2):
            picked = jnp.where(bin_of == b, right[q], jnp.zeros((), jnp.bfloat16))
            buffer[b, q] = jnp.dot(left[...], picked, preferred_element_type=jnp.float32).astype(jnp.bfloat16)
        copy(b).start()
        return carry

    lax.fori_loop(0, BINS, one_bin, 0, unroll=4)

    def done(b, carry):
        copy(b).wait()
        return carry

    lax.fori_loop(0, BINS, done, 0)


def local(traces, file_lengths, gap_starts, gap_lengths):
    smem = pl.BlockSpec(memory_space=pltpu.SMEM)
    vmem = pl.BlockSpec(memory_space=pltpu.VMEM)
    anywhere = pl.BlockSpec(memory_space=pl.ANY)
    dma = pltpu.SemaphoreType.DMA
    params = dict(vmem_limit_bytes=VMEM_LIMIT)
    table = jnp.asarray(dft_table())
    part = pl.pallas_call(
        dft_kernel,
        out_shape=jax.ShapeDtypeStruct((N_ROW, 128, LANES), jnp.float32),
        in_specs=[smem, anywhere, anywhere],
        out_specs=vmem,
        scratch_shapes=[
            pltpu.VMEM((CHUNKS, CHUNK, WINDOWS, FILE_MOST), jnp.bfloat16),
            pltpu.VMEM((CHUNKS, 2 * BINS, CHUNK * WINDOWS), jnp.bfloat16),
            dma((CHUNKS,)), dma((CHUNKS,)),
        ],
        compiler_params=pltpu.CompilerParams(**params),
        name="table_product",
    )(file_lengths, jnp.transpose(traces, (2, 1, 0)), table)
    left, right = pl.pallas_call(
        exchange_kernel,
        out_shape=(
            jax.ShapeDtypeStruct((4, FEATURES, LANES), jnp.bfloat16),
            jax.ShapeDtypeStruct((2, FEATURES, LANES), jnp.bfloat16),
        ),
        in_specs=[smem, smem, smem, vmem],
        out_specs=(vmem, vmem),
        scratch_shapes=[
            pltpu.VMEM((N_ROW - 1, 128, LANES), jnp.float32),
            pltpu.VMEM((2, 64, LANES), jnp.bfloat16),
            pltpu.VMEM((N_COL, 64, LANES), jnp.bfloat16),
            pltpu.VMEM((64, LANES), jnp.bfloat16),
            pltpu.VMEM((4, FEATURES, LANES), jnp.bfloat16),
            pltpu.VMEM((2, FEATURES, LANES), jnp.bfloat16),
            dma((N_ROW - 1,)), dma((N_ROW - 1,)),
            dma((N_COL - 1,)), dma((N_COL - 1,)),
            dma((N_COL,)), dma((N_COL,)),
            dma((N_ROW,)), dma((N_ROW,)),
            dma,
        ],
        compiler_params=pltpu.CompilerParams(collective_id=0, has_side_effects=True, **params),
        name="exchange",
    )(file_lengths, gap_starts, gap_lengths, part)
    return pl.pallas_call(
        cross_kernel,
        out_shape=jax.ShapeDtypeStruct((BINS, 2, FILE_MOST, 2 * LANES), jnp.bfloat16),
        in_specs=[vmem, vmem],
        out_specs=anywhere,
        scratch_shapes=[
            pltpu.VMEM((FILE_MOST, FEATURES), jnp.bfloat16),
            pltpu.VMEM((2, FEATURES, 2 * LANES), jnp.bfloat16),
            pltpu.VMEM((BINS, 2, FILE_MOST, 2 * LANES), jnp.bfloat16),
            dma((BINS,)),
        ],
        compiler_params=pltpu.CompilerParams(**params),
        name="cross",
    )(left, right)


def solution(mesh):
    in_specs = (P("col", None, "row"), P(), P(), P())
    out_specs = P(None, None, "row", "col")
    return jax.shard_map(local, mesh=mesh, in_specs=in_specs, out_specs=out_specs, check_vma=False)
```

```python
import math

import jax
import jax.numpy as jnp
import ml_dtypes
import numpy as np
from jax import lax
from jax.experimental import pallas as pl
from jax.experimental.pallas import tpu as pltpu
from jax.sharding import PartitionSpec as P

SAMPLES = 15000
BINS = 32
WINDOWS = 4
FILE_MOST = 512
N_COL = 16
N_ROW = 8
GAPS = 16
FEATURES = WINDOWS * 2 * BINS
LANES = 128
SLICE = SAMPLES // N_ROW
CHUNKS = 5
CHUNK = SLICE // CHUNKS
AHEAD = 3
TABLE_LANES = -(-CHUNK * WINDOWS // LANES) * LANES

lowest_bin = 60
bin_stride = 15
floor_level = 0.2
half_window = 2

VMEM_LIMIT = 60 << 20
MESH = pl.DeviceIdType.MESH


def dft_table():
    sample = np.arange(SAMPLES)
    wave = lowest_bin + bin_stride * np.arange(BINS)
    angle = (sample[:, None] * wave[None, :] % SAMPLES) * (2.0 * math.pi / SAMPLES)
    taper = 0.5 - 0.5 * np.cos(sample * (2.0 * math.pi / SAMPLES))
    weight = taper / math.sqrt(SAMPLES)
    table = np.concatenate([weight[:, None] * np.cos(angle), -weight[:, None] * np.sin(angle)], axis=1)
    table = table.astype(np.float32).astype(ml_dtypes.bfloat16)
    table = table.reshape(N_ROW, CHUNKS, CHUNK, 2 * BINS).transpose(0, 1, 3, 2)
    table = np.repeat(table, WINDOWS, axis=3)
    return np.pad(table, ((0, 0), (0, 0), (0, 0), (0, TABLE_LANES - CHUNK * WINDOWS)))


def file_bounds(lengths_ref):
    firsts, total = [], 0
    for f in range(N_COL):
        firsts.append(total)
        total = total + lengths_ref[f]
    return firsts + [total]


def whiten(total):
    bins = lax.broadcasted_iota(jnp.int32, (BINS, LANES), 0)
    low = jnp.minimum(bins, half_window)
    high = jnp.minimum(BINS - 1 - bins, half_window)
    counted = (low + high + 1).astype(jnp.float32)
    edge = jnp.zeros((8, LANES), jnp.float32)
    re = total[0:BINS]
    im = total[BINS : 2 * BINS]
    magnitude = jnp.sqrt(re * re + im * im)
    padded = jnp.concatenate([edge, magnitude, edge], axis=0)
    running = padded[8 - half_window : 8 - half_window + BINS]
    for offset in range(1 - half_window, half_window + 1):
        running = running + padded[8 + offset : 8 + offset + BINS]
    level = running / counted
    factor = 1.0 / jnp.maximum(level, floor_level)
    return jnp.concatenate([re * factor, im * factor], axis=0)


def exchange_kernel(
    lengths_ref, gap_starts_ref, gap_lengths_ref, x_hbm, table_hbm, left_ref, right_ref,
    xs, ts, parts, sums, picked, got, block, rows, cols,
    x_sem, t_sem, send1, recv1, send2, recv2, send3, recv3, send4, recv4,
):
    row, col = lax.axis_index("row"), lax.axis_index("col")
    z = row // 2
    half = row % 2
    side = col % 2
    k = col // 2

    def copies(c):
        return (
            pltpu.make_async_copy(table_hbm.at[row, c], ts.at[c], t_sem.at[c]),
            pltpu.make_async_copy(x_hbm.at[pl.ds(c * CHUNK, CHUNK)], xs.at[c], x_sem.at[c]),
        )

    for c in range(AHEAD):
        for copy in copies(c):
            copy.start()

    across = [(d, s) for d in range(N_ROW) for s in range(2) if (d, s) != (0, 0)]

    def row_peer(d, s):
        return (row + d) % N_ROW, 2 * k + (side + s) % 2

    def col_peer(d):
        return row, 2 * ((k + d) % 8) + side

    barrier = pltpu.get_barrier_semaphore()
    for d, s in across:
        pl.semaphore_signal(barrier, inc=1, device_id=row_peer(d, s), device_id_type=MESH)
    for d in range(1, 8):
        pl.semaphore_signal(barrier, inc=1, device_id=col_peer(d), device_id_type=MESH)

    total = None
    for c in range(CHUNKS):
        for copy in copies(c):
            copy.wait()
        if c + AHEAD < CHUNKS:
            for copy in copies(c + AHEAD):
                copy.start()
        table = ts[c, :, 0 : CHUNK * WINDOWS]
        window = lax.broadcasted_iota(jnp.int32, table.shape, 1) % WINDOWS
        wide = jnp.concatenate(
            [jnp.where(window == w, table, jnp.zeros_like(table)) for w in range(WINDOWS)], axis=0
        )
        samples = xs[c].reshape(CHUNK * WINDOWS, FILE_MOST)
        part = jnp.dot(wide, samples, preferred_element_type=jnp.float32)
        total = part if total is None else total + part
    bounds = file_bounds(lengths_ref)
    first = 0
    for f in range(N_COL):
        first = first + jnp.where(f < col, lengths_ref[f], 0)
    turned = pltpu.roll(total, lax.rem(first, FILE_MOST), axis=1)
    for w in range(WINDOWS):
        for q in range(4):
            parts[w, q] = turned[64 * w : 64 * w + 64, LANES * q : LANES * q + LANES]
    pl.semaphore_wait(barrier, len(across) + 7)

    def copy1(i):
        there, lane = row_peer(*across[i])
        window, quarter = 2 * (there % 2) + lane % 2, there // 2
        return pltpu.make_async_remote_copy(
            src_ref=parts.at[window, quarter], dst_ref=sums.at[2 * row + side],
            send_sem=send1.at[i], recv_sem=recv1.at[2 * row + side],
            device_id=(there, lane), device_id_type=MESH,
        )

    for i in range(len(across)):
        copy1(i).start()
    sums[2 * row + side] = parts[2 * half + side, z]
    lane = lax.broadcasted_iota(jnp.int32, (1, LANES), 1)
    low = [0, 0]
    high = [0, 0]
    for f in range(N_COL):
        low[f % 2] = jnp.where(f // 2 == k, bounds[f], low[f % 2])
        high[f % 2] = jnp.where(f // 2 == k, bounds[f + 1], high[f % 2])
    choice = []
    for q in range(8):
        channel = FILE_MOST * q + LANES * z + lane
        dead = jnp.zeros((1, LANES), jnp.bool_)
        for g in range(GAPS):
            gap = gap_starts_ref[g]
            dead = dead | ((channel >= gap) & (channel < gap + gap_lengths_ref[g]))
        live = jnp.where(dead, 0.0, 1.0)
        choice.append([
            jnp.where((channel >= low[s]) & (channel < high[s]), live, 0.0) for s in range(2)
        ])
    for d, s in across:
        there, lane_peer = row_peer(d, s)
        slot = 2 * there + lane_peer % 2
        pltpu.make_async_copy(sums.at[slot], sums.at[slot], recv1.at[slot]).wait()
    white = []
    for s in range(2):
        total = sums[s]
        for r in range(1, N_ROW):
            total = total + sums[2 * r + s]
        white.append(whiten(total))
    for q in range(8):
        merged = jnp.where(choice[q][0] > 0.0, white[0], jnp.where(choice[q][1] > 0.0, white[1], 0.0))
        picked[q] = merged.astype(jnp.bfloat16)

    def copy2(d):
        there = col_peer(d)
        return pltpu.make_async_remote_copy(
            src_ref=picked.at[(k + d) % 8], dst_ref=got.at[k],
            send_sem=send2.at[d - 1], recv_sem=recv2.at[k],
            device_id=there, device_id_type=MESH,
        )

    for d in range(1, 8):
        copy2(d).start()
    got[k] = picked[k]
    for d in range(1, 8):
        slot = (k + d) % 8
        pltpu.make_async_copy(got.at[slot], got.at[slot], recv2.at[slot]).wait()
    whole = got[0].astype(jnp.float32)
    for q in range(1, 8):
        whole = whole + got[q].astype(jnp.float32)
    block[...] = whole.astype(jnp.bfloat16)

    at = pl.multiple_of((2 * half + side) * 64, 64)
    lane_block = z % 2
    near = 2 * k + z // 2

    def copy3(d):
        there = (col + d) % N_COL
        return pltpu.make_async_remote_copy(
            src_ref=block, dst_ref=rows.at[z, pl.ds(at, 64)],
            send_sem=send3.at[d], recv_sem=recv3.at[row * 2 + side],
            device_id=(k, there), device_id_type=MESH,
        )

    def copy4(d):
        there = (row + d) % N_ROW
        return pltpu.make_async_remote_copy(
            src_ref=block, dst_ref=cols.at[lane_block, pl.ds(at, 64)],
            send_sem=send4.at[d], recv_sem=recv4.at[lane_block * 4 + half * 2 + side],
            device_id=(there, near), device_id_type=MESH,
        )

    for d in range(1, N_COL):
        copy3(d).start()
    for d in range(1, N_ROW):
        copy4(d).start()

    @pl.when(row != k)
    def _():
        copy3(0).start()

    @pl.when(row == k)
    def _():
        rows[z, pl.ds(at, 64)] = block[...]

    @pl.when(near != col)
    def _():
        copy4(0).start()

    @pl.when(near == col)
    def _():
        cols[lane_block, pl.ds(at, 64)] = block[...]

    for i in range(len(across)):
        copy1(i).wait_send()
    for d in range(1, 8):
        copy2(d).wait_send()
    for d in range(1, N_COL):
        copy3(d).wait_send()
    for d in range(1, N_ROW):
        copy4(d).wait_send()

    @pl.when(row != k)
    def _():
        copy3(0).wait_send()

    @pl.when(near != col)
    def _():
        copy4(0).wait_send()

    for source_row in range(N_ROW):
        for s in range(2):
            @pl.when(jnp.logical_or(row != source_row, col != 2 * row + s))
            def _():
                pltpu.make_async_copy(block, rows.at[0, pl.ds(0, 64)], recv3.at[source_row * 2 + s]).wait()
    for q in range(2):
        for h in range(2):
            for s in range(2):
                @pl.when(jnp.logical_or(row != 2 * (2 * side + q) + h, side != s))
                def _():
                    pltpu.make_async_copy(block, cols.at[0, pl.ds(0, 64)], recv4.at[q * 4 + h * 2 + s]).wait()
    left_ref[...] = rows[...]
    right_ref[...] = cols[...]


def cross_kernel(left_ref, right_ref, out_hbm, left, right, buffer, sem):
    for z in range(4):
        left[LANES * z : LANES * z + LANES, :] = left_ref[z].astype(jnp.float32).T.astype(jnp.bfloat16)
    for q in range(2):
        part = right_ref[q] * jnp.asarray(1.0 / WINDOWS, jnp.bfloat16)
        right[0, :, LANES * q : LANES * q + LANES] = part
        for w in range(WINDOWS):
            re = part[64 * w : 64 * w + BINS]
            im = part[64 * w + BINS : 64 * w + 2 * BINS]
            right[1, 64 * w : 64 * w + BINS, LANES * q : LANES * q + LANES] = -im
            right[1, 64 * w + BINS : 64 * w + 2 * BINS, LANES * q : LANES * q + LANES] = re
    bin_of = lax.broadcasted_iota(jnp.int32, (FEATURES, 2 * LANES), 0) % BINS

    def copy(b):
        return pltpu.make_async_copy(buffer.at[b], out_hbm.at[b], sem.at[b])

    def one_bin(b, carry):
        for q in range(2):
            picked = jnp.where(bin_of == b, right[q], jnp.zeros((), jnp.bfloat16))
            buffer[b, q] = jnp.dot(left[...], picked, preferred_element_type=jnp.float32).astype(jnp.bfloat16)
        copy(b).start()
        return carry

    lax.fori_loop(0, BINS, one_bin, 0, unroll=4)

    def done(b, carry):
        copy(b).wait()
        return carry

    lax.fori_loop(0, BINS, done, 0)


def local(traces, file_lengths, gap_starts, gap_lengths):
    smem = pl.BlockSpec(memory_space=pltpu.SMEM)
    vmem = pl.BlockSpec(memory_space=pltpu.VMEM)
    anywhere = pl.BlockSpec(memory_space=pl.ANY)
    dma = pltpu.SemaphoreType.DMA
    params = dict(vmem_limit_bytes=VMEM_LIMIT)
    table = jnp.asarray(dft_table())
    left, right = pl.pallas_call(
        exchange_kernel,
        out_shape=(
            jax.ShapeDtypeStruct((4, FEATURES, LANES), jnp.bfloat16),
            jax.ShapeDtypeStruct((2, FEATURES, LANES), jnp.bfloat16),
        ),
        in_specs=[smem, smem, smem, anywhere, anywhere],
        out_specs=(vmem, vmem),
        scratch_shapes=[
            pltpu.VMEM((CHUNKS, CHUNK, WINDOWS, FILE_MOST), jnp.bfloat16),
            pltpu.VMEM((CHUNKS, 2 * BINS, TABLE_LANES), jnp.bfloat16),
            pltpu.VMEM((WINDOWS, 4, 64, LANES), jnp.float32),
            pltpu.VMEM((2 * N_ROW, 64, LANES), jnp.float32),
            pltpu.VMEM((8, 64, LANES), jnp.bfloat16),
            pltpu.VMEM((8, 64, LANES), jnp.bfloat16),
            pltpu.VMEM((64, LANES), jnp.bfloat16),
            pltpu.VMEM((4, FEATURES, LANES), jnp.bfloat16),
            pltpu.VMEM((2, FEATURES, LANES), jnp.bfloat16),
            dma((CHUNKS,)), dma((CHUNKS,)),
            dma((2 * N_ROW - 1,)), dma((2 * N_ROW,)),
            dma((7,)), dma((8,)),
            dma((N_COL,)), dma((N_COL,)),
            dma((N_ROW,)), dma((N_ROW,)),
        ],
        compiler_params=pltpu.CompilerParams(collective_id=0, has_side_effects=True, **params),
        name="exchange",
    )(file_lengths, gap_starts, gap_lengths, jnp.transpose(traces, (2, 1, 0)), table)
    return pl.pallas_call(
        cross_kernel,
        out_shape=jax.ShapeDtypeStruct((BINS, 2, FILE_MOST, 2 * LANES), jnp.bfloat16),
        in_specs=[vmem, vmem],
        out_specs=anywhere,
        scratch_shapes=[
            pltpu.VMEM((FILE_MOST, FEATURES), jnp.bfloat16),
            pltpu.VMEM((2, FEATURES, 2 * LANES), jnp.bfloat16),
            pltpu.VMEM((BINS, 2, FILE_MOST, 2 * LANES), jnp.bfloat16),
            dma((BINS,)),
        ],
        compiler_params=pltpu.CompilerParams(**params),
        name="cross",
    )(left, right)


def solution(mesh):
    in_specs = (P("col", None, "row"), P(), P(), P())
    out_specs = P(None, None, "row", "col")
    return jax.shard_map(local, mesh=mesh, in_specs=in_specs, out_specs=out_specs, check_vma=False)
```

```python
import math

import jax
import jax.numpy as jnp
import ml_dtypes
import numpy as np
from jax import lax
from jax.experimental import pallas as pl
from jax.experimental.pallas import tpu as pltpu
from jax.sharding import PartitionSpec as P

SAMPLES = 15000
BINS = 32
WINDOWS = 4
FILE_MOST = 512
N_COL = 16
N_ROW = 8
GAPS = 16
FEATURES = WINDOWS * 2 * BINS
LANES = 128
SLICE = SAMPLES // N_ROW
CHUNKS = 5
CHUNK = SLICE // CHUNKS
AHEAD = 3
HAND_ON = 4
TABLE_LANES = -(-CHUNK * WINDOWS // LANES) * LANES

lowest_bin = 60
bin_stride = 15
floor_level = 0.2
half_window = 2

EXCHANGE_VMEM = 48 << 20
CROSS_VMEM = 24 << 20
MESH = pl.DeviceIdType.MESH


def dft_table():
    sample = np.arange(SAMPLES)
    wave = lowest_bin + bin_stride * np.arange(BINS)
    angle = (sample[:, None] * wave[None, :] % SAMPLES) * (2.0 * math.pi / SAMPLES)
    taper = 0.5 - 0.5 * np.cos(sample * (2.0 * math.pi / SAMPLES))
    weight = taper / math.sqrt(SAMPLES)
    table = np.concatenate([weight[:, None] * np.cos(angle), -weight[:, None] * np.sin(angle)], axis=1)
    table = table.astype(np.float32).astype(ml_dtypes.bfloat16)
    table = table.reshape(N_ROW, CHUNKS, CHUNK, 2 * BINS).transpose(0, 1, 3, 2)
    table = np.repeat(table, WINDOWS, axis=3)
    return np.pad(table, ((0, 0), (0, 0), (0, 0), (0, TABLE_LANES - CHUNK * WINDOWS)))


def file_bounds(lengths_ref):
    firsts, total = [], 0
    for f in range(N_COL):
        firsts.append(total)
        total = total + lengths_ref[f]
    return firsts + [total]


def whiten(total):
    bins = lax.broadcasted_iota(jnp.int32, (BINS, LANES), 0)
    low = jnp.minimum(bins, half_window)
    high = jnp.minimum(BINS - 1 - bins, half_window)
    counted = (low + high + 1).astype(jnp.float32)
    edge = jnp.zeros((8, LANES), jnp.float32)
    re = total[0:BINS]
    im = total[BINS : 2 * BINS]
    magnitude = jnp.sqrt(re * re + im * im)
    padded = jnp.concatenate([edge, magnitude, edge], axis=0)
    running = padded[8 - half_window : 8 - half_window + BINS]
    for offset in range(1 - half_window, half_window + 1):
        running = running + padded[8 + offset : 8 + offset + BINS]
    level = running / counted
    factor = 1.0 / jnp.maximum(level, floor_level)
    return jnp.concatenate([re * factor, im * factor], axis=0)


def exchange_kernel(
    lengths_hbm, gap_starts_hbm, gap_lengths_hbm, x_hbm, table_hbm, left_ref, right_ref,
    lengths_ref, gap_starts_ref, gap_lengths_ref, xs, ts, parts, sums, picked, got, block, rows, cols,
    small_sem, x_sem, t_sem, send1, recv1, send2, recv2, send3, recv3, send4, recv4, send5, recv5,
):
    row, col = lax.axis_index("row"), lax.axis_index("col")
    z = row // 2
    half = row % 2
    side = col % 2
    k = col // 2

    def copies(c):
        return (
            pltpu.make_async_copy(table_hbm.at[row, c], ts.at[c], t_sem.at[c]),
            pltpu.make_async_copy(x_hbm.at[pl.ds(c * CHUNK, CHUNK)], xs.at[c], x_sem.at[c]),
        )

    for c in range(AHEAD):
        for copy in copies(c):
            copy.start()

    across = [(d, s) for d in range(N_ROW) for s in range(2) if (d, s) != (0, 0)]

    def row_peer(d, s):
        return (row + d) % N_ROW, 2 * k + (side + s) % 2

    def col_peer(d):
        return row, 2 * ((k + d) % 8) + side

    barrier = pltpu.get_barrier_semaphore()
    for d, s in across:
        pl.semaphore_signal(barrier, inc=1, device_id=row_peer(d, s), device_id_type=MESH)
    for d in range(1, 8):
        pl.semaphore_signal(barrier, inc=1, device_id=col_peer(d), device_id_type=MESH)

    small = [
        pltpu.make_async_copy(lengths_hbm, lengths_ref, small_sem.at[0]),
        pltpu.make_async_copy(gap_starts_hbm, gap_starts_ref, small_sem.at[1]),
        pltpu.make_async_copy(gap_lengths_hbm, gap_lengths_ref, small_sem.at[2]),
    ]
    for copy in small:
        copy.start()

    total = None
    for c in range(CHUNKS):
        for copy in copies(c):
            copy.wait()
        if c + AHEAD < CHUNKS:
            for copy in copies(c + AHEAD):
                copy.start()
        table = ts[c, :, 0 : CHUNK * WINDOWS]
        window = lax.broadcasted_iota(jnp.int32, table.shape, 1) % WINDOWS
        wide = jnp.concatenate(
            [jnp.where(window == w, table, jnp.zeros_like(table)) for w in range(WINDOWS)], axis=0
        )
        samples = xs[c].reshape(CHUNK * WINDOWS, FILE_MOST)
        part = jnp.dot(wide, samples, preferred_element_type=jnp.float32)
        total = part if total is None else total + part
    for copy in small:
        copy.wait()
    bounds = file_bounds(lengths_ref)
    first = 0
    for f in range(N_COL):
        first = first + jnp.where(f < col, lengths_ref[f], 0)
    turned = pltpu.roll(total, lax.rem(first, FILE_MOST), axis=1)
    for w in range(WINDOWS):
        for q in range(4):
            parts[w, q] = turned[64 * w : 64 * w + 64, LANES * q : LANES * q + LANES]
    pl.semaphore_wait(barrier, len(across) + 7)

    def copy1(i):
        there, lane = row_peer(*across[i])
        window, quarter = 2 * (there % 2) + lane % 2, there // 2
        return pltpu.make_async_remote_copy(
            src_ref=parts.at[window, quarter], dst_ref=sums.at[2 * row + side],
            send_sem=send1.at[i], recv_sem=recv1.at[2 * row + side],
            device_id=(there, lane), device_id_type=MESH,
        )

    for i in range(len(across)):
        copy1(i).start()
    sums[2 * row + side] = parts[2 * half + side, z]
    lane = lax.broadcasted_iota(jnp.int32, (1, LANES), 1)
    low = [0, 0]
    high = [0, 0]
    for f in range(N_COL):
        low[f % 2] = jnp.where(f // 2 == k, bounds[f], low[f % 2])
        high[f % 2] = jnp.where(f // 2 == k, bounds[f + 1], high[f % 2])
    choice = []
    for q in range(8):
        channel = FILE_MOST * q + LANES * z + lane
        dead = jnp.zeros((1, LANES), jnp.bool_)
        for g in range(GAPS):
            gap = gap_starts_ref[g]
            dead = dead | ((channel >= gap) & (channel < gap + gap_lengths_ref[g]))
        live = jnp.where(dead, 0.0, 1.0)
        choice.append([
            jnp.where((channel >= low[s]) & (channel < high[s]), live, 0.0) for s in range(2)
        ])
    for d, s in across:
        there, lane_peer = row_peer(d, s)
        slot = 2 * there + lane_peer % 2
        pltpu.make_async_copy(sums.at[slot], sums.at[slot], recv1.at[slot]).wait()
    white = []
    for s in range(2):
        total = sums[s]
        for r in range(1, N_ROW):
            total = total + sums[2 * r + s]
        white.append(whiten(total))
    for q in range(8):
        merged = jnp.where(choice[q][0] > 0.0, white[0], jnp.where(choice[q][1] > 0.0, white[1], 0.0))
        picked[q] = merged.astype(jnp.bfloat16)

    def copy2(d):
        there = col_peer(d)
        return pltpu.make_async_remote_copy(
            src_ref=picked.at[(k + d) % 8], dst_ref=got.at[k],
            send_sem=send2.at[d - 1], recv_sem=recv2.at[k],
            device_id=there, device_id_type=MESH,
        )

    for d in range(1, 8):
        copy2(d).start()
    got[k] = picked[k]
    for d in range(1, 8):
        slot = (k + d) % 8
        pltpu.make_async_copy(got.at[slot], got.at[slot], recv2.at[slot]).wait()
    whole = got[0].astype(jnp.float32)
    for q in range(1, 8):
        whole = whole + got[q].astype(jnp.float32)
    block[...] = whole.astype(jnp.bfloat16)

    near = 2 * k + z // 2
    at = pl.multiple_of((2 * side + half) * 64, 64)

    def copy3(d):
        return pltpu.make_async_remote_copy(
            src_ref=block, dst_ref=rows.at[side, z, half],
            send_sem=send3.at[d], recv_sem=recv3.at[row],
            device_id=(k, 2 * ((k + d) % 8) + side), device_id_type=MESH,
        )

    def copy4(d):
        there = (row + d) % N_ROW
        return pltpu.make_async_remote_copy(
            src_ref=block, dst_ref=cols.at[z % 2, pl.ds(at, 64)],
            send_sem=send4.at[d], recv_sem=recv4.at[(z % 2) * 4 + half * 2 + side],
            device_id=(there, near), device_id_type=MESH,
        )

    def copy5(h):
        some = rows.at[side, pl.ds(h * HAND_ON, HAND_ON)]
        return pltpu.make_async_remote_copy(
            src_ref=some, dst_ref=some, send_sem=send5.at[h], recv_sem=recv5.at[h],
            device_id=(row, 2 * k + 1 - side), device_id_type=MESH,
        )

    for d in range(1, 8):
        copy3(d).start()

    @pl.when(row != k)
    def _():
        copy3(0).start()

    @pl.when(row == k)
    def _():
        rows[side, z, half] = block[...]

    for d in range(1, N_ROW):
        copy4(d).start()

    @pl.when(near != col)
    def _():
        copy4(0).start()

    @pl.when(near == col)
    def _():
        cols[z % 2, pl.ds(at, 64)] = block[...]

    for source in range(N_ROW):
        @pl.when(jnp.logical_or(row != source, k != row))
        def _():
            pltpu.make_async_copy(block, rows.at[side, source // 2, source % 2], recv3.at[source]).wait()
        if source % (2 * HAND_ON) == 2 * HAND_ON - 1:
            copy5(source // (2 * HAND_ON)).start()
    for q in range(2):
        for h in range(2):
            for s in range(2):
                @pl.when(jnp.logical_or(row != 2 * (2 * side + q) + h, side != s))
                def _():
                    pltpu.make_async_copy(block, cols.at[0, pl.ds(0, 64)], recv4.at[q * 4 + h * 2 + s]).wait()
    right_ref[...] = cols[...]
    for i in range(len(across)):
        copy1(i).wait_send()
    for d in range(1, 8):
        copy2(d).wait_send()
        copy3(d).wait_send()
        copy4(d).wait_send()

    @pl.when(row != k)
    def _():
        copy3(0).wait_send()

    @pl.when(near != col)
    def _():
        copy4(0).wait_send()

    for h in range(4 // HAND_ON):
        copy5(h).wait()
    left_ref[...] = rows[...]


def cross_kernel(left_ref, right_ref, out_hbm, left, right, buffer, sem):
    for z in range(4):
        for side in range(2):
            some = left_ref[side, z].reshape(LANES, LANES).astype(jnp.float32).T.astype(jnp.bfloat16)
            left[LANES * z : LANES * z + LANES, LANES * side : LANES * side + LANES] = some
    for q in range(2):
        part = right_ref[q] * jnp.asarray(1.0 / WINDOWS, jnp.bfloat16)
        right[0, :, LANES * q : LANES * q + LANES] = part
        for w in range(WINDOWS):
            re = part[64 * w : 64 * w + BINS]
            im = part[64 * w + BINS : 64 * w + 2 * BINS]
            right[1, 64 * w : 64 * w + BINS, LANES * q : LANES * q + LANES] = -im
            right[1, 64 * w + BINS : 64 * w + 2 * BINS, LANES * q : LANES * q + LANES] = re
    bin_of = lax.broadcasted_iota(jnp.int32, (FEATURES, 2 * LANES), 0) % BINS

    def copy(b):
        return pltpu.make_async_copy(buffer.at[b], out_hbm.at[b], sem.at[b])

    def one_bin(b, carry):
        for q in range(2):
            picked = jnp.where(bin_of == b, right[q], jnp.zeros((), jnp.bfloat16))
            buffer[b, q] = jnp.dot(left[...], picked, preferred_element_type=jnp.float32).astype(jnp.bfloat16)
        copy(b).start()
        return carry

    lax.fori_loop(0, BINS, one_bin, 0, unroll=32)

    def done(b, carry):
        copy(b).wait()
        return carry

    lax.fori_loop(0, BINS, done, 0)


def local(traces, file_lengths, gap_starts, gap_lengths):
    vmem = pl.BlockSpec(memory_space=pltpu.VMEM)
    anywhere = pl.BlockSpec(memory_space=pltpu.HBM)
    dma = pltpu.SemaphoreType.DMA
    table = jnp.asarray(dft_table())
    left, right = pl.pallas_call(
        exchange_kernel,
        out_shape=(
            jax.ShapeDtypeStruct((2, 4, 2, 64, LANES), jnp.bfloat16),
            jax.ShapeDtypeStruct((2, FEATURES, LANES), jnp.bfloat16),
        ),
        in_specs=[anywhere] * 5,
        out_specs=(vmem, vmem),
        scratch_shapes=[
            pltpu.SMEM((N_COL,), jnp.int32), pltpu.SMEM((GAPS,), jnp.int32), pltpu.SMEM((GAPS,), jnp.int32),
            pltpu.VMEM((CHUNKS, CHUNK, WINDOWS, FILE_MOST), jnp.bfloat16),
            pltpu.VMEM((CHUNKS, 2 * BINS, TABLE_LANES), jnp.bfloat16),
            pltpu.VMEM((WINDOWS, 4, 64, LANES), jnp.float32),
            pltpu.VMEM((2 * N_ROW, 64, LANES), jnp.float32),
            pltpu.VMEM((8, 64, LANES), jnp.bfloat16),
            pltpu.VMEM((8, 64, LANES), jnp.bfloat16),
            pltpu.VMEM((64, LANES), jnp.bfloat16),
            pltpu.VMEM((2, 4, 2, 64, LANES), jnp.bfloat16),
            pltpu.VMEM((2, FEATURES, LANES), jnp.bfloat16),
            dma((3,)), dma((CHUNKS,)), dma((CHUNKS,)),
            dma((2 * N_ROW - 1,)), dma((2 * N_ROW,)),
            dma((7,)), dma((8,)),
            dma((8,)), dma((8,)),
            dma((N_ROW,)), dma((N_ROW,)),
            dma((4 // HAND_ON,)), dma((4 // HAND_ON,)),
        ],
        compiler_params=pltpu.CompilerParams(collective_id=0, has_side_effects=True, vmem_limit_bytes=EXCHANGE_VMEM),
        name="exchange",
    )(*[pltpu.with_memory_space_constraint(v, pltpu.HBM) for v in (file_lengths, gap_starts, gap_lengths, jnp.transpose(traces, (2, 1, 0)), table)])
    return pl.pallas_call(
        cross_kernel,
        out_shape=jax.ShapeDtypeStruct((BINS, 2, FILE_MOST, 2 * LANES), jnp.bfloat16),
        in_specs=[vmem, vmem],
        out_specs=anywhere,
        scratch_shapes=[
            pltpu.VMEM((FILE_MOST, FEATURES), jnp.bfloat16),
            pltpu.VMEM((2, FEATURES, 2 * LANES), jnp.bfloat16),
            pltpu.VMEM((BINS, 2, FILE_MOST, 2 * LANES), jnp.bfloat16),
            dma((BINS,)),
        ],
        compiler_params=pltpu.CompilerParams(vmem_limit_bytes=CROSS_VMEM),
        name="cross",
    )(left, right)


def solution(mesh):
    in_specs = (P("col", None, "row"), P(), P(), P())
    out_specs = P(None, None, "row", "col")
    return jax.shard_map(local, mesh=mesh, in_specs=in_specs, out_specs=out_specs, check_vma=False)
```

```python
import math

import jax
import jax.numpy as jnp
import ml_dtypes
import numpy as np
from jax import lax
from jax.experimental import pallas as pl
from jax.experimental.pallas import tpu as pltpu
from jax.sharding import PartitionSpec as P

SAMPLES = 15000
BINS = 32
WINDOWS = 4
FILE_MOST = 512
N_COL = 16
N_ROW = 8
GAPS = 16
FEATURES = WINDOWS * 2 * BINS
LANES = 128
SLICE = SAMPLES // N_ROW
CHUNKS = 5
CHUNK = SLICE // CHUNKS
AHEAD = 3
HAND_ON = 4
TABLE_LANES = -(-CHUNK * WINDOWS // LANES) * LANES

lowest_bin = 60
bin_stride = 15
floor_level = 0.2
half_window = 2

EXCHANGE_VMEM = 48 << 20
CROSS_VMEM = 24 << 20
MESH = pl.DeviceIdType.MESH


def dft_table():
    sample = np.arange(SAMPLES)
    wave = lowest_bin + bin_stride * np.arange(BINS)
    angle = (sample[:, None] * wave[None, :] % SAMPLES) * (2.0 * math.pi / SAMPLES)
    taper = 0.5 - 0.5 * np.cos(sample * (2.0 * math.pi / SAMPLES))
    weight = taper / math.sqrt(SAMPLES)
    table = np.concatenate([weight[:, None] * np.cos(angle), -weight[:, None] * np.sin(angle)], axis=1)
    table = table.astype(np.float32).astype(ml_dtypes.bfloat16)
    table = table.reshape(N_ROW, CHUNKS, CHUNK, 2 * BINS).transpose(0, 1, 3, 2)
    table = np.repeat(table, WINDOWS, axis=3)
    return np.pad(table, ((0, 0), (0, 0), (0, 0), (0, TABLE_LANES - CHUNK * WINDOWS)))


def file_bounds(lengths_ref):
    firsts, total = [], 0
    for f in range(N_COL):
        firsts.append(total)
        total = total + lengths_ref[f]
    return firsts + [total]


def whiten(total):
    bins = lax.broadcasted_iota(jnp.int32, (BINS, LANES), 0)
    low = jnp.minimum(bins, half_window)
    high = jnp.minimum(BINS - 1 - bins, half_window)
    counted = (low + high + 1).astype(jnp.float32)
    edge = jnp.zeros((8, LANES), jnp.float32)
    re = total[0:BINS]
    im = total[BINS : 2 * BINS]
    magnitude = jnp.sqrt(re * re + im * im)
    padded = jnp.concatenate([edge, magnitude, edge], axis=0)
    running = padded[8 - half_window : 8 - half_window + BINS]
    for offset in range(1 - half_window, half_window + 1):
        running = running + padded[8 + offset : 8 + offset + BINS]
    level = running / counted
    factor = 1.0 / jnp.maximum(level, floor_level)
    return jnp.concatenate([re * factor, im * factor], axis=0)


def exchange_kernel(
    lengths_hbm, gap_starts_hbm, gap_lengths_hbm, x_hbm, table_hbm, left_ref, right_ref,
    lengths_ref, gap_starts_ref, gap_lengths_ref, xs, ts, parts, sums, picked, got, block, rows, cols,
    small_sem, x_sem, t_sem, send1, recv1, send2, recv2, send3, recv3, send4, recv4, send5, recv5,
):
    row, col = lax.axis_index("row"), lax.axis_index("col")
    z = row // 2
    half = row % 2
    side = col % 2
    k = col // 2

    def copies(c):
        return (
            pltpu.make_async_copy(table_hbm.at[row, c], ts.at[c], t_sem.at[c]),
            pltpu.make_async_copy(x_hbm.at[pl.ds(c * CHUNK, CHUNK)], xs.at[c], x_sem.at[c]),
        )

    for c in range(AHEAD):
        for copy in copies(c):
            copy.start()

    across = [(d, s) for d in range(N_ROW) for s in range(2) if (d, s) != (0, 0)]

    def row_peer(d, s):
        return (row + d) % N_ROW, 2 * k + (side + s) % 2

    def col_peer(d):
        return row, 2 * ((k + d) % 8) + side

    barrier = pltpu.get_barrier_semaphore()
    for d, s in across:
        pl.semaphore_signal(barrier, inc=1, device_id=row_peer(d, s), device_id_type=MESH)
    for d in range(1, 8):
        pl.semaphore_signal(barrier, inc=1, device_id=col_peer(d), device_id_type=MESH)

    small = [
        pltpu.make_async_copy(lengths_hbm, lengths_ref, small_sem.at[0]),
        pltpu.make_async_copy(gap_starts_hbm, gap_starts_ref, small_sem.at[1]),
        pltpu.make_async_copy(gap_lengths_hbm, gap_lengths_ref, small_sem.at[2]),
    ]
    for copy in small:
        copy.start()

    total = None
    for c in range(CHUNKS):
        for copy in copies(c):
            copy.wait()
        if c + AHEAD < CHUNKS:
            for copy in copies(c + AHEAD):
                copy.start()
        table = ts[c, :, 0 : CHUNK * WINDOWS]
        window = lax.broadcasted_iota(jnp.int32, table.shape, 1) % WINDOWS
        wide = jnp.concatenate(
            [jnp.where(window == w, table, jnp.zeros_like(table)) for w in range(WINDOWS)], axis=0
        )
        samples = xs[c].reshape(CHUNK * WINDOWS, FILE_MOST)
        part = jnp.dot(wide, samples, preferred_element_type=jnp.float32)
        total = part if total is None else total + part
    for copy in small:
        copy.wait()
    bounds = file_bounds(lengths_ref)
    first = 0
    for f in range(N_COL):
        first = first + jnp.where(f < col, lengths_ref[f], 0)
    turn = lax.rem(first, FILE_MOST)
    pl.semaphore_wait(barrier, len(across) + 7)

    def copy1(w, d):
        there = 2 * ((z + d) % 4) + w // 2
        return pltpu.make_async_remote_copy(
            src_ref=parts.at[w, (z + d) % 4], dst_ref=sums.at[2 * row + side],
            send_sem=send1.at[4 * w + d], recv_sem=recv1.at[2 * row + side],
            device_id=(there, 2 * k + w % 2), device_id_type=MESH,
        )

    own = 2 * half + side
    for w in range(WINDOWS):
        turned = pltpu.roll(total[64 * w : 64 * w + 64], turn, axis=1)
        for q in range(4):
            parts[w, q] = turned[:, LANES * q : LANES * q + LANES]
        for d in (1, 3, 2):
            copy1(w, d).start()

        @pl.when(w != own)
        def _():
            copy1(w, 0).start()

        @pl.when(w == own)
        def _():
            sums[2 * row + side] = parts[w, z]
    lane = lax.broadcasted_iota(jnp.int32, (1, LANES), 1)
    low = [0, 0]
    high = [0, 0]
    for f in range(N_COL):
        low[f % 2] = jnp.where(f // 2 == k, bounds[f], low[f % 2])
        high[f % 2] = jnp.where(f // 2 == k, bounds[f + 1], high[f % 2])
    choice = []
    for q in range(8):
        channel = FILE_MOST * q + LANES * z + lane
        dead = jnp.zeros((1, LANES), jnp.bool_)
        for g in range(GAPS):
            gap = gap_starts_ref[g]
            dead = dead | ((channel >= gap) & (channel < gap + gap_lengths_ref[g]))
        live = jnp.where(dead, 0.0, 1.0)
        choice.append([
            jnp.where((channel >= low[s]) & (channel < high[s]), live, 0.0) for s in range(2)
        ])
    for d, s in across:
        there, lane_peer = row_peer(d, s)
        slot = 2 * there + lane_peer % 2
        pltpu.make_async_copy(sums.at[slot], sums.at[slot], recv1.at[slot]).wait()
    white = []
    for s in range(2):
        total = sums[s]
        for r in range(1, N_ROW):
            total = total + sums[2 * r + s]
        white.append(whiten(total))
    for q in range(8):
        merged = jnp.where(choice[q][0] > 0.0, white[0], jnp.where(choice[q][1] > 0.0, white[1], 0.0))
        picked[q] = merged.astype(jnp.bfloat16)

    def copy2(d):
        there = col_peer(d)
        return pltpu.make_async_remote_copy(
            src_ref=picked.at[(k + d) % 8], dst_ref=got.at[k],
            send_sem=send2.at[d - 1], recv_sem=recv2.at[k],
            device_id=there, device_id_type=MESH,
        )

    for d in range(1, 8):
        copy2(d).start()
    got[k] = picked[k]
    for d in range(1, 8):
        slot = (k + d) % 8
        pltpu.make_async_copy(got.at[slot], got.at[slot], recv2.at[slot]).wait()
    whole = got[0].astype(jnp.float32)
    for q in range(1, 8):
        whole = whole + got[q].astype(jnp.float32)
    block[...] = whole.astype(jnp.bfloat16)

    near = 2 * k + z // 2
    at = pl.multiple_of((2 * side + half) * 64, 64)

    def copy3(d):
        return pltpu.make_async_remote_copy(
            src_ref=block, dst_ref=rows.at[side, z, half],
            send_sem=send3.at[d], recv_sem=recv3.at[row],
            device_id=(k, 2 * ((k + d) % 8) + side), device_id_type=MESH,
        )

    def copy4(d):
        there = (row + d) % N_ROW
        return pltpu.make_async_remote_copy(
            src_ref=block, dst_ref=cols.at[z % 2, pl.ds(at, 64)],
            send_sem=send4.at[d], recv_sem=recv4.at[(z % 2) * 4 + half * 2 + side],
            device_id=(there, near), device_id_type=MESH,
        )

    def copy5(h):
        some = rows.at[side, pl.ds(h * HAND_ON, HAND_ON)]
        return pltpu.make_async_remote_copy(
            src_ref=some, dst_ref=some, send_sem=send5.at[h], recv_sem=recv5.at[h],
            device_id=(row, 2 * k + 1 - side), device_id_type=MESH,
        )

    for d in range(1, 8):
        copy3(d).start()

    @pl.when(row != k)
    def _():
        copy3(0).start()

    @pl.when(row == k)
    def _():
        rows[side, z, half] = block[...]

    for d in range(1, N_ROW):
        copy4(d).start()

    @pl.when(near != col)
    def _():
        copy4(0).start()

    @pl.when(near == col)
    def _():
        cols[z % 2, pl.ds(at, 64)] = block[...]

    for source in range(N_ROW):
        @pl.when(jnp.logical_or(row != source, k != row))
        def _():
            pltpu.make_async_copy(block, rows.at[side, source // 2, source % 2], recv3.at[source]).wait()
        if source % (2 * HAND_ON) == 2 * HAND_ON - 1:
            copy5(source // (2 * HAND_ON)).start()
    def turn_block(which):
        at_lane = pl.ds(pl.multiple_of(LANES * which, LANES), LANES)
        for q in range(4):
            some = rows[which, q].reshape(LANES, LANES).astype(jnp.float32)
            left_ref[LANES * q : LANES * q + LANES, at_lane] = some.T.astype(jnp.bfloat16)

    turn_block(side)
    for q in range(2):
        for h in range(2):
            for s in range(2):
                @pl.when(jnp.logical_or(row != 2 * (2 * side + q) + h, side != s))
                def _():
                    pltpu.make_async_copy(block, cols.at[0, pl.ds(0, 64)], recv4.at[q * 4 + h * 2 + s]).wait()
    for q in range(2):
        lanes = pl.ds(LANES * q, LANES)
        part = cols[q] * jnp.asarray(1.0 / WINDOWS, jnp.bfloat16)
        right_ref[0, :, lanes] = part
        for w in range(WINDOWS):
            right_ref[1, 64 * w : 64 * w + BINS, lanes] = -part[64 * w + BINS : 64 * w + 2 * BINS]
            right_ref[1, 64 * w + BINS : 64 * w + 2 * BINS, lanes] = part[64 * w : 64 * w + BINS]
    for w in range(WINDOWS):
        for d in range(1, 4):
            copy1(w, d).wait_send()

        @pl.when(w != own)
        def _():
            copy1(w, 0).wait_send()

    for d in range(1, 8):
        copy2(d).wait_send()
        copy3(d).wait_send()
        copy4(d).wait_send()

    @pl.when(row != k)
    def _():
        copy3(0).wait_send()

    @pl.when(near != col)
    def _():
        copy4(0).wait_send()

    for h in range(4 // HAND_ON):
        copy5(h).wait()
    turn_block(1 - side)


def cross_kernel(left_ref, right_ref, out_hbm, buffer, sem):
    bin_of = lax.broadcasted_iota(jnp.int32, (FEATURES, 2 * LANES), 0) % BINS

    def copy(b):
        return pltpu.make_async_copy(buffer.at[b], out_hbm.at[b], sem.at[b])

    def one_bin(b, carry):
        for q in range(2):
            picked = jnp.where(bin_of == b, right_ref[q], jnp.zeros((), jnp.bfloat16))
            buffer[b, q] = jnp.dot(left_ref[...], picked, preferred_element_type=jnp.float32).astype(jnp.bfloat16)
        copy(b).start()
        return carry

    lax.fori_loop(0, BINS, one_bin, 0, unroll=32)

    def done(b, carry):
        copy(b).wait()
        return carry

    lax.fori_loop(0, BINS, done, 0)


def local(traces, file_lengths, gap_starts, gap_lengths):
    vmem = pl.BlockSpec(memory_space=pltpu.VMEM)
    anywhere = pl.BlockSpec(memory_space=pltpu.HBM)
    dma = pltpu.SemaphoreType.DMA
    table = jnp.asarray(dft_table())
    left, right = pl.pallas_call(
        exchange_kernel,
        out_shape=(
            jax.ShapeDtypeStruct((FILE_MOST, FEATURES), jnp.bfloat16),
            jax.ShapeDtypeStruct((2, FEATURES, 2 * LANES), jnp.bfloat16),
        ),
        in_specs=[anywhere] * 5,
        out_specs=(vmem, vmem),
        scratch_shapes=[
            pltpu.SMEM((N_COL,), jnp.int32), pltpu.SMEM((GAPS,), jnp.int32), pltpu.SMEM((GAPS,), jnp.int32),
            pltpu.VMEM((CHUNKS, CHUNK, WINDOWS, FILE_MOST), jnp.bfloat16),
            pltpu.VMEM((CHUNKS, 2 * BINS, TABLE_LANES), jnp.bfloat16),
            pltpu.VMEM((WINDOWS, 4, 64, LANES), jnp.float32),
            pltpu.VMEM((2 * N_ROW, 64, LANES), jnp.float32),
            pltpu.VMEM((8, 64, LANES), jnp.bfloat16),
            pltpu.VMEM((8, 64, LANES), jnp.bfloat16),
            pltpu.VMEM((64, LANES), jnp.bfloat16),
            pltpu.VMEM((2, 4, 2, 64, LANES), jnp.bfloat16),
            pltpu.VMEM((2, FEATURES, LANES), jnp.bfloat16),
            dma((3,)), dma((CHUNKS,)), dma((CHUNKS,)),
            dma((4 * WINDOWS,)), dma((2 * N_ROW,)),
            dma((7,)), dma((8,)),
            dma((8,)), dma((8,)),
            dma((N_ROW,)), dma((N_ROW,)),
            dma((4 // HAND_ON,)), dma((4 // HAND_ON,)),
        ],
        compiler_params=pltpu.CompilerParams(collective_id=0, has_side_effects=True, vmem_limit_bytes=EXCHANGE_VMEM),
        name="exchange",
    )(*[pltpu.with_memory_space_constraint(v, pltpu.HBM) for v in (file_lengths, gap_starts, gap_lengths, jnp.transpose(traces, (2, 1, 0)), table)])
    return pl.pallas_call(
        cross_kernel,
        out_shape=jax.ShapeDtypeStruct((BINS, 2, FILE_MOST, 2 * LANES), jnp.bfloat16),
        in_specs=[vmem, vmem],
        out_specs=anywhere,
        scratch_shapes=[
            pltpu.VMEM((BINS, 2, FILE_MOST, 2 * LANES), jnp.bfloat16),
            dma((BINS,)),
        ],
        compiler_params=pltpu.CompilerParams(vmem_limit_bytes=CROSS_VMEM),
        name="cross",
    )(left, right)


def solution(mesh):
    in_specs = (P("col", None, "row"), P(), P(), P())
    out_specs = P(None, None, "row", "col")
    return jax.shard_map(local, mesh=mesh, in_specs=in_specs, out_specs=out_specs, check_vma=False)
```

```python
import math

import jax
import jax.numpy as jnp
import ml_dtypes
import numpy as np
from jax import lax
from jax.experimental import pallas as pl
from jax.experimental.pallas import tpu as pltpu
from jax.sharding import PartitionSpec as P

SAMPLES = 15000
BINS = 32
WINDOWS = 4
FILE_MOST = 512
N_COL = 16
N_ROW = 8
GAPS = 16
FEATURES = WINDOWS * 2 * BINS
LANES = 128
SLICE = SAMPLES // N_ROW
CHUNKS = 5
CHUNK = SLICE // CHUNKS
AHEAD = 3
HAND_ON = 4
TABLE_LANES = -(-CHUNK * WINDOWS // LANES) * LANES

lowest_bin = 60
bin_stride = 15
floor_level = 0.2
half_window = 2

EXCHANGE_VMEM = 48 << 20
CROSS_VMEM = 24 << 20
MESH = pl.DeviceIdType.MESH


def dft_table():
    sample = np.arange(SAMPLES)
    wave = lowest_bin + bin_stride * np.arange(BINS)
    angle = (sample[:, None] * wave[None, :] % SAMPLES) * (2.0 * math.pi / SAMPLES)
    taper = 0.5 - 0.5 * np.cos(sample * (2.0 * math.pi / SAMPLES))
    weight = taper / math.sqrt(SAMPLES)
    table = np.concatenate([weight[:, None] * np.cos(angle), -weight[:, None] * np.sin(angle)], axis=1)
    table = table.astype(np.float32).astype(ml_dtypes.bfloat16)
    table = table.reshape(N_ROW, CHUNKS, CHUNK, 2 * BINS).transpose(0, 1, 3, 2)
    table = np.repeat(table, WINDOWS, axis=3)
    return np.pad(table, ((0, 0), (0, 0), (0, 0), (0, TABLE_LANES - CHUNK * WINDOWS)))


def file_bounds(lengths_ref):
    firsts, total = [], 0
    for f in range(N_COL):
        firsts.append(total)
        total = total + lengths_ref[f]
    return firsts + [total]


def whiten(total):
    bins = lax.broadcasted_iota(jnp.int32, (BINS, LANES), 0)
    low = jnp.minimum(bins, half_window)
    high = jnp.minimum(BINS - 1 - bins, half_window)
    counted = (low + high + 1).astype(jnp.float32)
    edge = jnp.zeros((8, LANES), jnp.float32)
    re = total[0:BINS]
    im = total[BINS : 2 * BINS]
    magnitude = jnp.sqrt(re * re + im * im)
    padded = jnp.concatenate([edge, magnitude, edge], axis=0)
    running = padded[8 - half_window : 8 - half_window + BINS]
    for offset in range(1 - half_window, half_window + 1):
        running = running + padded[8 + offset : 8 + offset + BINS]
    level = running / counted
    factor = 1.0 / jnp.maximum(level, floor_level)
    return jnp.concatenate([re * factor, im * factor], axis=0)


def exchange_kernel(
    lengths_hbm, gap_starts_hbm, gap_lengths_hbm, x_hbm, table_hbm, left_ref, right_ref,
    lengths_ref, gap_starts_ref, gap_lengths_ref, xs, ts, parts, sums, picked, got, block, rows, cols,
    small_sem, x_sem, t_sem, send1, recv1, send2, recv2, send3, recv3, send4, recv4, send5, recv5,
):
    row, col = lax.axis_index("row"), lax.axis_index("col")
    z = row // 2
    half = row % 2
    side = col % 2
    k = col // 2

    def copies(c):
        return (
            pltpu.make_async_copy(table_hbm.at[row, c], ts.at[c], t_sem.at[c]),
            pltpu.make_async_copy(x_hbm.at[pl.ds(c * CHUNK, CHUNK)], xs.at[c], x_sem.at[c]),
        )

    for c in range(AHEAD):
        for copy in copies(c):
            copy.start()

    across = [(d, s) for d in range(N_ROW) for s in range(2) if (d, s) != (0, 0)]

    def row_peer(d, s):
        return (row + d) % N_ROW, 2 * k + (side + s) % 2

    def col_peer(d):
        return row, 2 * ((k + d) % 8) + side

    barrier = pltpu.get_barrier_semaphore()
    for d, s in across:
        pl.semaphore_signal(barrier, inc=1, device_id=row_peer(d, s), device_id_type=MESH)
    for d in range(1, 8):
        pl.semaphore_signal(barrier, inc=1, device_id=col_peer(d), device_id_type=MESH)

    small = [
        pltpu.make_async_copy(lengths_hbm, lengths_ref, small_sem.at[0]),
        pltpu.make_async_copy(gap_starts_hbm, gap_starts_ref, small_sem.at[1]),
        pltpu.make_async_copy(gap_lengths_hbm, gap_lengths_ref, small_sem.at[2]),
    ]
    for copy in small:
        copy.start()

    total = None
    for c in range(CHUNKS):
        for copy in copies(c):
            copy.wait()
        if c + AHEAD < CHUNKS:
            for copy in copies(c + AHEAD):
                copy.start()
        table = ts[c, :, 0 : CHUNK * WINDOWS]
        window = lax.broadcasted_iota(jnp.int32, table.shape, 1) % WINDOWS
        wide = jnp.concatenate(
            [jnp.where(window == w, table, jnp.zeros_like(table)) for w in range(WINDOWS)], axis=0
        )
        samples = xs[c].reshape(CHUNK * WINDOWS, FILE_MOST)
        part = jnp.dot(wide, samples, preferred_element_type=jnp.float32)
        total = part if total is None else total + part
    for copy in small:
        copy.wait()
    bounds = file_bounds(lengths_ref)
    first = 0
    for f in range(N_COL):
        first = first + jnp.where(f < col, lengths_ref[f], 0)
    turn = lax.rem(first, FILE_MOST)
    pl.semaphore_wait(barrier, len(across) + 7)

    def copy1(w, d):
        there = 2 * ((z + d) % 4) + w // 2
        return pltpu.make_async_remote_copy(
            src_ref=parts.at[w, (z + d) % 4], dst_ref=sums.at[2 * row + side],
            send_sem=send1.at[4 * w + d], recv_sem=recv1.at[2 * row + side],
            device_id=(there, 2 * k + w % 2), device_id_type=MESH,
        )

    own = 2 * half + side
    for w in (0, 2, 1, 3):
        turned = pltpu.roll(total[64 * w : 64 * w + 64], turn, axis=1)
        for q in range(4):
            parts[w, q] = turned[:, LANES * q : LANES * q + LANES]
        for d in (1, 3, 2):
            copy1(w, d).start()

        @pl.when(w != own)
        def _():
            copy1(w, 0).start()

        @pl.when(w == own)
        def _():
            sums[2 * row + side] = parts[w, z]
    lane = lax.broadcasted_iota(jnp.int32, (1, LANES), 1)
    low = [0, 0]
    high = [0, 0]
    for f in range(N_COL):
        low[f % 2] = jnp.where(f // 2 == k, bounds[f], low[f % 2])
        high[f % 2] = jnp.where(f // 2 == k, bounds[f + 1], high[f % 2])
    choice = []
    for q in range(8):
        channel = FILE_MOST * q + LANES * z + lane
        dead = jnp.zeros((1, LANES), jnp.bool_)
        for g in range(GAPS):
            gap = gap_starts_ref[g]
            dead = dead | ((channel >= gap) & (channel < gap + gap_lengths_ref[g]))
        live = jnp.where(dead, 0.0, 1.0)
        choice.append([
            jnp.where((channel >= low[s]) & (channel < high[s]), live, 0.0) for s in range(2)
        ])
    for d, s in across:
        there, lane_peer = row_peer(d, s)
        slot = 2 * there + lane_peer % 2
        pltpu.make_async_copy(sums.at[slot], sums.at[slot], recv1.at[slot]).wait()
    white = []
    for s in range(2):
        total = sums[s]
        for r in range(1, N_ROW):
            total = total + sums[2 * r + s]
        white.append(whiten(total))
    for q in range(8):
        merged = jnp.where(choice[q][0] > 0.0, white[0], jnp.where(choice[q][1] > 0.0, white[1], 0.0))
        picked[q] = merged.astype(jnp.bfloat16)

    def copy2(d):
        there = col_peer(d)
        return pltpu.make_async_remote_copy(
            src_ref=picked.at[(k + d) % 8], dst_ref=got.at[k],
            send_sem=send2.at[d - 1], recv_sem=recv2.at[k],
            device_id=there, device_id_type=MESH,
        )

    for d in range(1, 8):
        copy2(d).start()
    got[k] = picked[k]
    for d in range(1, 8):
        slot = (k + d) % 8
        pltpu.make_async_copy(got.at[slot], got.at[slot], recv2.at[slot]).wait()
    whole = got[0].astype(jnp.float32)
    for q in range(1, 8):
        whole = whole + got[q].astype(jnp.float32)
    block[...] = whole.astype(jnp.bfloat16)

    near = 2 * k + z // 2
    at = pl.multiple_of((2 * side + half) * 64, 64)

    def copy3(d):
        return pltpu.make_async_remote_copy(
            src_ref=block, dst_ref=rows.at[side, z, half],
            send_sem=send3.at[d], recv_sem=recv3.at[row],
            device_id=(k, 2 * ((k + d) % 8) + side), device_id_type=MESH,
        )

    def copy4(d):
        there = (row + d) % N_ROW
        return pltpu.make_async_remote_copy(
            src_ref=block, dst_ref=cols.at[z % 2, pl.ds(at, 64)],
            send_sem=send4.at[d], recv_sem=recv4.at[(z % 2) * 4 + half * 2 + side],
            device_id=(there, near), device_id_type=MESH,
        )

    def copy5(h):
        some = rows.at[side, pl.ds(h * HAND_ON, HAND_ON)]
        return pltpu.make_async_remote_copy(
            src_ref=some, dst_ref=some, send_sem=send5.at[h], recv_sem=recv5.at[h],
            device_id=(row, 2 * k + 1 - side), device_id_type=MESH,
        )

    for x_step, y_step in ((1, 0), (3, 0), (0, 1), (1, 1), (3, 1), (2, 0), (2, 1)):
        there = 4 * ((k // 4 + y_step) % 2) + (k % 4 + x_step) % 4
        copy3(lax.rem(there - k + 8, 8)).start()

    @pl.when(row != k)
    def _():
        copy3(0).start()

    @pl.when(row == k)
    def _():
        rows[side, z, half] = block[...]

    for d in range(1, N_ROW):
        copy4(d).start()

    @pl.when(near != col)
    def _():
        copy4(0).start()

    @pl.when(near == col)
    def _():
        cols[z % 2, pl.ds(at, 64)] = block[...]

    for source in range(N_ROW):
        @pl.when(jnp.logical_or(row != source, k != row))
        def _():
            pltpu.make_async_copy(block, rows.at[side, source // 2, source % 2], recv3.at[source]).wait()
        if source % (2 * HAND_ON) == 2 * HAND_ON - 1:
            copy5(source // (2 * HAND_ON)).start()
    def turn_block(which):
        at_lane = pl.ds(pl.multiple_of(LANES * which, LANES), LANES)
        for q in range(4):
            some = rows[which, q].reshape(LANES, LANES).astype(jnp.float32)
            left_ref[LANES * q : LANES * q + LANES, at_lane] = some.T.astype(jnp.bfloat16)

    turn_block(side)
    for q in range(2):
        for h in range(2):
            for s in range(2):
                @pl.when(jnp.logical_or(row != 2 * (2 * side + q) + h, side != s))
                def _():
                    pltpu.make_async_copy(block, cols.at[0, pl.ds(0, 64)], recv4.at[q * 4 + h * 2 + s]).wait()
    for q in range(2):
        lanes = pl.ds(LANES * q, LANES)
        part = cols[q] * jnp.asarray(1.0 / WINDOWS, jnp.bfloat16)
        right_ref[0, :, lanes] = part
        for w in range(WINDOWS):
            right_ref[1, 64 * w : 64 * w + BINS, lanes] = -part[64 * w + BINS : 64 * w + 2 * BINS]
            right_ref[1, 64 * w + BINS : 64 * w + 2 * BINS, lanes] = part[64 * w : 64 * w + BINS]
    for w in range(WINDOWS):
        for d in range(1, 4):
            copy1(w, d).wait_send()

        @pl.when(w != own)
        def _():
            copy1(w, 0).wait_send()

    for d in range(1, 8):
        copy2(d).wait_send()
        copy3(d).wait_send()
        copy4(d).wait_send()

    @pl.when(row != k)
    def _():
        copy3(0).wait_send()

    @pl.when(near != col)
    def _():
        copy4(0).wait_send()

    for h in range(4 // HAND_ON):
        copy5(h).wait()
    turn_block(1 - side)


def cross_kernel(left_ref, right_ref, out_hbm, buffer, sem):
    bin_of = lax.broadcasted_iota(jnp.int32, (FEATURES, 2 * LANES), 0) % BINS

    def copy(b):
        return pltpu.make_async_copy(buffer.at[b], out_hbm.at[b], sem.at[b])

    def one_bin(b, carry):
        for q in range(2):
            picked = jnp.where(bin_of == b, right_ref[q], jnp.zeros((), jnp.bfloat16))
            buffer[b, q] = jnp.dot(left_ref[...], picked, preferred_element_type=jnp.float32).astype(jnp.bfloat16)
        copy(b).start()
        return carry

    lax.fori_loop(0, BINS, one_bin, 0, unroll=32)

    def done(b, carry):
        copy(b).wait()
        return carry

    lax.fori_loop(0, BINS, done, 0)


def local(traces, file_lengths, gap_starts, gap_lengths):
    vmem = pl.BlockSpec(memory_space=pltpu.VMEM)
    anywhere = pl.BlockSpec(memory_space=pltpu.HBM)
    dma = pltpu.SemaphoreType.DMA
    table = jnp.asarray(dft_table())
    left, right = pl.pallas_call(
        exchange_kernel,
        out_shape=(
            jax.ShapeDtypeStruct((FILE_MOST, FEATURES), jnp.bfloat16),
            jax.ShapeDtypeStruct((2, FEATURES, 2 * LANES), jnp.bfloat16),
        ),
        in_specs=[anywhere] * 5,
        out_specs=(vmem, vmem),
        scratch_shapes=[
            pltpu.SMEM((N_COL,), jnp.int32), pltpu.SMEM((GAPS,), jnp.int32), pltpu.SMEM((GAPS,), jnp.int32),
            pltpu.VMEM((CHUNKS, CHUNK, WINDOWS, FILE_MOST), jnp.bfloat16),
            pltpu.VMEM((CHUNKS, 2 * BINS, TABLE_LANES), jnp.bfloat16),
            pltpu.VMEM((WINDOWS, 4, 64, LANES), jnp.float32),
            pltpu.VMEM((2 * N_ROW, 64, LANES), jnp.float32),
            pltpu.VMEM((8, 64, LANES), jnp.bfloat16),
            pltpu.VMEM((8, 64, LANES), jnp.bfloat16),
            pltpu.VMEM((64, LANES), jnp.bfloat16),
            pltpu.VMEM((2, 4, 2, 64, LANES), jnp.bfloat16),
            pltpu.VMEM((2, FEATURES, LANES), jnp.bfloat16),
            dma((3,)), dma((CHUNKS,)), dma((CHUNKS,)),
            dma((4 * WINDOWS,)), dma((2 * N_ROW,)),
            dma((7,)), dma((8,)),
            dma((8,)), dma((8,)),
            dma((N_ROW,)), dma((N_ROW,)),
            dma((4 // HAND_ON,)), dma((4 // HAND_ON,)),
        ],
        compiler_params=pltpu.CompilerParams(collective_id=0, has_side_effects=True, vmem_limit_bytes=EXCHANGE_VMEM),
        name="exchange",
    )(*[pltpu.with_memory_space_constraint(v, pltpu.HBM) for v in (file_lengths, gap_starts, gap_lengths, jnp.transpose(traces, (2, 1, 0)), table)])
    return pl.pallas_call(
        cross_kernel,
        out_shape=jax.ShapeDtypeStruct((BINS, 2, FILE_MOST, 2 * LANES), jnp.bfloat16),
        in_specs=[vmem, vmem],
        out_specs=anywhere,
        scratch_shapes=[
            pltpu.VMEM((BINS, 2, FILE_MOST, 2 * LANES), jnp.bfloat16),
            dma((BINS,)),
        ],
        compiler_params=pltpu.CompilerParams(vmem_limit_bytes=CROSS_VMEM),
        name="cross",
    )(left, right)


def solution(mesh):
    in_specs = (P("col", None, "row"), P(), P(), P())
    out_specs = P(None, None, "row", "col")
    return jax.shard_map(local, mesh=mesh, in_specs=in_specs, out_specs=out_specs, check_vma=False)
```

```python
import math

import jax
import jax.numpy as jnp
import ml_dtypes
import numpy as np
from jax import lax
from jax.experimental import pallas as pl
from jax.experimental.pallas import tpu as pltpu
from jax.sharding import PartitionSpec as P

SAMPLES = 15000
BINS = 32
WINDOWS = 4
FILE_MOST = 512
N_COL = 16
N_ROW = 8
GAPS = 16
FEATURES = WINDOWS * 2 * BINS
LANES = 128
SLICE = SAMPLES // N_ROW
CHUNKS = 5
CHUNK = SLICE // CHUNKS
AHEAD = 3
HAND_ON = 4
TABLE_LANES = -(-CHUNK * WINDOWS // LANES) * LANES

lowest_bin = 60
bin_stride = 15
floor_level = 0.2
half_window = 2

EXCHANGE_VMEM = 48 << 20
CROSS_VMEM = 24 << 20
MESH = pl.DeviceIdType.MESH


def dft_table():
    sample = np.arange(SAMPLES)
    wave = lowest_bin + bin_stride * np.arange(BINS)
    angle = (sample[:, None] * wave[None, :] % SAMPLES) * (2.0 * math.pi / SAMPLES)
    taper = 0.5 - 0.5 * np.cos(sample * (2.0 * math.pi / SAMPLES))
    weight = taper / math.sqrt(SAMPLES)
    table = np.concatenate([weight[:, None] * np.cos(angle), -weight[:, None] * np.sin(angle)], axis=1)
    table = table.astype(np.float32).astype(ml_dtypes.bfloat16)
    table = table.reshape(N_ROW, CHUNKS, CHUNK, 2 * BINS).transpose(0, 1, 3, 2)
    table = np.repeat(table, WINDOWS, axis=3)
    return np.pad(table, ((0, 0), (0, 0), (0, 0), (0, TABLE_LANES - CHUNK * WINDOWS)))


def file_bounds(lengths_ref):
    firsts, total = [], 0
    for f in range(N_COL):
        firsts.append(total)
        total = total + lengths_ref[f]
    return firsts + [total]


def whiten(total):
    bins = lax.broadcasted_iota(jnp.int32, (BINS, LANES), 0)
    low = jnp.minimum(bins, half_window)
    high = jnp.minimum(BINS - 1 - bins, half_window)
    counted = (low + high + 1).astype(jnp.float32)
    edge = jnp.zeros((8, LANES), jnp.float32)
    re = total[0:BINS]
    im = total[BINS : 2 * BINS]
    magnitude = jnp.sqrt(re * re + im * im)
    padded = jnp.concatenate([edge, magnitude, edge], axis=0)
    running = padded[8 - half_window : 8 - half_window + BINS]
    for offset in range(1 - half_window, half_window + 1):
        running = running + padded[8 + offset : 8 + offset + BINS]
    level = running / counted
    factor = 1.0 / jnp.maximum(level, floor_level)
    return jnp.concatenate([re * factor, im * factor], axis=0)


def exchange_kernel(
    lengths_hbm, gap_starts_hbm, gap_lengths_hbm, x_hbm, table_hbm, left_ref, right_ref,
    lengths_ref, gap_starts_ref, gap_lengths_ref, xs, ts, parts, sums, picked, got, block, rows, cols,
    small_sem, x_sem, t_sem, send1, recv1, send2, recv2, send3, recv3, send4, recv4, send5, recv5,
):
    row, col = lax.axis_index("row"), lax.axis_index("col")
    z = row // 2
    half = row % 2
    side = col % 2
    k = col // 2

    def copies(c):
        return (
            pltpu.make_async_copy(table_hbm.at[row, c], ts.at[c], t_sem.at[c]),
            pltpu.make_async_copy(x_hbm.at[pl.ds(c * CHUNK, CHUNK)], xs.at[c], x_sem.at[c]),
        )

    for c in range(AHEAD):
        for copy in copies(c):
            copy.start()

    across = [(d, s) for d in range(N_ROW) for s in range(2) if (d, s) != (0, 0)]

    def row_peer(d, s):
        return (row + d) % N_ROW, 2 * k + (side + s) % 2

    def col_peer(d):
        return row, 2 * ((k + d) % 8) + side

    barrier = pltpu.get_barrier_semaphore()
    for d, s in across:
        pl.semaphore_signal(barrier, inc=1, device_id=row_peer(d, s), device_id_type=MESH)
    for d in range(1, 8):
        pl.semaphore_signal(barrier, inc=1, device_id=col_peer(d), device_id_type=MESH)

    small = [
        pltpu.make_async_copy(lengths_hbm, lengths_ref, small_sem.at[0]),
        pltpu.make_async_copy(gap_starts_hbm, gap_starts_ref, small_sem.at[1]),
        pltpu.make_async_copy(gap_lengths_hbm, gap_lengths_ref, small_sem.at[2]),
    ]
    for copy in small:
        copy.start()

    total = None
    for c in range(CHUNKS):
        for copy in copies(c):
            copy.wait()
        if c + AHEAD < CHUNKS:
            for copy in copies(c + AHEAD):
                copy.start()
        table = ts[c, :, 0 : CHUNK * WINDOWS]
        window = lax.broadcasted_iota(jnp.int32, table.shape, 1) % WINDOWS
        wide = jnp.concatenate(
            [jnp.where(window == w, table, jnp.zeros_like(table)) for w in range(WINDOWS)], axis=0
        )
        samples = xs[c].reshape(CHUNK * WINDOWS, FILE_MOST)
        part = jnp.dot(wide, samples, preferred_element_type=jnp.float32)
        total = part if total is None else total + part
    for copy in small:
        copy.wait()
    bounds = file_bounds(lengths_ref)
    first = 0
    for f in range(N_COL):
        first = first + jnp.where(f < col, lengths_ref[f], 0)
    turn = lax.rem(first, FILE_MOST)
    pl.semaphore_wait(barrier, len(across) + 7)

    def copy1(w, d):
        there = 2 * ((z + d) % 4) + w // 2
        return pltpu.make_async_remote_copy(
            src_ref=parts.at[w, (z + d) % 4], dst_ref=sums.at[2 * row + side],
            send_sem=send1.at[4 * w + d], recv_sem=recv1.at[2 * row + side],
            device_id=(there, 2 * k + w % 2), device_id_type=MESH,
        )

    own = 2 * half + side
    for w in (0, 2, 1, 3):
        turned = pltpu.roll(total[64 * w : 64 * w + 64], turn, axis=1)
        for q in range(4):
            parts[w, q] = turned[:, LANES * q : LANES * q + LANES]
        for d in (1, 3, 2):
            copy1(w, d).start()

        @pl.when(w != own)
        def _():
            copy1(w, 0).start()

        @pl.when(w == own)
        def _():
            sums[2 * row + side] = parts[w, z]
    lane = lax.broadcasted_iota(jnp.int32, (1, LANES), 1)
    low = [0, 0]
    high = [0, 0]
    for f in range(N_COL):
        low[f % 2] = jnp.where(f // 2 == k, bounds[f], low[f % 2])
        high[f % 2] = jnp.where(f // 2 == k, bounds[f + 1], high[f % 2])
    choice = []
    for q in range(8):
        channel = FILE_MOST * q + LANES * z + lane
        dead = jnp.zeros((1, LANES), jnp.bool_)
        for g in range(GAPS):
            gap = gap_starts_ref[g]
            dead = dead | ((channel >= gap) & (channel < gap + gap_lengths_ref[g]))
        live = jnp.where(dead, 0.0, 1.0)
        choice.append([
            jnp.where((channel >= low[s]) & (channel < high[s]), live, 0.0) for s in range(2)
        ])
    for d, s in across:
        there, lane_peer = row_peer(d, s)
        slot = 2 * there + lane_peer % 2
        pltpu.make_async_copy(sums.at[slot], sums.at[slot], recv1.at[slot]).wait()
    white = []
    for s in range(2):
        total = sums[s]
        for r in range(1, N_ROW):
            total = total + sums[2 * r + s]
        white.append(whiten(total))
    for q in range(8):
        merged = jnp.where(choice[q][0] > 0.0, white[0], jnp.where(choice[q][1] > 0.0, white[1], 0.0))
        picked[q] = merged.astype(jnp.bfloat16)

    def copy2(d):
        there = col_peer(d)
        return pltpu.make_async_remote_copy(
            src_ref=picked.at[(k + d) % 8], dst_ref=got.at[k],
            send_sem=send2.at[d - 1], recv_sem=recv2.at[k],
            device_id=there, device_id_type=MESH,
        )

    for d in range(1, 8):
        copy2(d).start()
    got[k] = picked[k]
    for d in range(1, 8):
        slot = (k + d) % 8
        pltpu.make_async_copy(got.at[slot], got.at[slot], recv2.at[slot]).wait()
    whole = got[0].astype(jnp.float32)
    for q in range(1, 8):
        whole = whole + got[q].astype(jnp.float32)
    block[...] = whole.astype(jnp.bfloat16)

    near = 2 * k + z // 2
    at = pl.multiple_of((2 * side + half) * 64, 64)

    def copy3(d):
        return pltpu.make_async_remote_copy(
            src_ref=block, dst_ref=rows.at[side, z, half],
            send_sem=send3.at[d], recv_sem=recv3.at[row],
            device_id=(k, 2 * ((k + d) % 8) + side), device_id_type=MESH,
        )

    def copy4(d):
        there = (row + d) % N_ROW
        return pltpu.make_async_remote_copy(
            src_ref=block, dst_ref=cols.at[z % 2, pl.ds(at, 64)],
            send_sem=send4.at[d], recv_sem=recv4.at[(z % 2) * 4 + half * 2 + side],
            device_id=(there, near), device_id_type=MESH,
        )

    def copy5(h):
        some = rows.at[side, pl.ds(h * HAND_ON, HAND_ON)]
        return pltpu.make_async_remote_copy(
            src_ref=some, dst_ref=some, send_sem=send5.at[h], recv_sem=recv5.at[h],
            device_id=(row, 2 * k + 1 - side), device_id_type=MESH,
        )

    for x_step, y_step in ((1, 0), (3, 0), (0, 1), (1, 1), (3, 1), (2, 0), (2, 1)):
        there = 4 * ((k // 4 + y_step) % 2) + (k % 4 + x_step) % 4
        copy3(lax.rem(there - k + 8, 8)).start()

    @pl.when(row != k)
    def _():
        copy3(0).start()

    @pl.when(row == k)
    def _():
        rows[side, z, half] = block[...]

    for d in range(1, N_ROW):
        copy4(d).start()

    @pl.when(near != col)
    def _():
        copy4(0).start()

    @pl.when(near == col)
    def _():
        cols[z % 2, pl.ds(at, 64)] = block[...]

    for source in range(N_ROW):
        @pl.when(jnp.logical_or(row != source, k != row))
        def _():
            pltpu.make_async_copy(block, rows.at[side, source // 2, source % 2], recv3.at[source]).wait()
        if source % (2 * HAND_ON) == 2 * HAND_ON - 1:
            copy5(source // (2 * HAND_ON)).start()
    def turn_block(which):
        at_lane = pl.ds(pl.multiple_of(LANES * which, LANES), LANES)
        for q in range(4):
            some = rows[which, q].reshape(LANES, LANES).astype(jnp.float32)
            left_ref[LANES * q : LANES * q + LANES, at_lane] = some.T.astype(jnp.bfloat16)

    turn_block(side)
    for q in range(2):
        for h in range(2):
            for s in range(2):
                @pl.when(jnp.logical_or(row != 2 * (2 * side + q) + h, side != s))
                def _():
                    pltpu.make_async_copy(block, cols.at[0, pl.ds(0, 64)], recv4.at[q * 4 + h * 2 + s]).wait()
    for q in range(2):
        lanes = pl.ds(LANES * q, LANES)
        part = cols[q] * jnp.asarray(1.0 / WINDOWS, jnp.bfloat16)
        right_ref[0, :, lanes] = part
        for w in range(WINDOWS):
            right_ref[1, 64 * w : 64 * w + BINS, lanes] = -part[64 * w + BINS : 64 * w + 2 * BINS]
            right_ref[1, 64 * w + BINS : 64 * w + 2 * BINS, lanes] = part[64 * w : 64 * w + BINS]
    for w in range(WINDOWS):
        for d in range(1, 4):
            copy1(w, d).wait_send()

        @pl.when(w != own)
        def _():
            copy1(w, 0).wait_send()

    for d in range(1, 8):
        copy2(d).wait_send()
        copy3(d).wait_send()
        copy4(d).wait_send()

    @pl.when(row != k)
    def _():
        copy3(0).wait_send()

    @pl.when(near != col)
    def _():
        copy4(0).wait_send()

    for h in range(4 // HAND_ON):
        copy5(h).wait()
    turn_block(1 - side)


def cross_kernel(left_ref, right_ref, out_hbm, buffer, sem):
    bin_of = lax.broadcasted_iota(jnp.int32, (FEATURES, 2 * LANES), 0) % BINS

    def copy(b, q):
        return pltpu.make_async_copy(buffer.at[b, q], out_hbm.at[b, q], sem.at[b, q])

    def one_bin(b, carry):
        for q in range(2):
            picked = jnp.where(bin_of == b, right_ref[q], jnp.zeros((), jnp.bfloat16))
            buffer[b, q] = jnp.dot(left_ref[...], picked, preferred_element_type=jnp.float32).astype(jnp.bfloat16)
            copy(b, q).start()
        return carry

    lax.fori_loop(0, BINS, one_bin, 0, unroll=32)

    def done(b, carry):
        copy(b, 0).wait()
        copy(b, 1).wait()
        return carry

    lax.fori_loop(0, BINS, done, 0)


def local(traces, file_lengths, gap_starts, gap_lengths):
    vmem = pl.BlockSpec(memory_space=pltpu.VMEM)
    anywhere = pl.BlockSpec(memory_space=pltpu.HBM)
    dma = pltpu.SemaphoreType.DMA
    table = jnp.asarray(dft_table())
    left, right = pl.pallas_call(
        exchange_kernel,
        out_shape=(
            jax.ShapeDtypeStruct((FILE_MOST, FEATURES), jnp.bfloat16),
            jax.ShapeDtypeStruct((2, FEATURES, 2 * LANES), jnp.bfloat16),
        ),
        in_specs=[anywhere] * 5,
        out_specs=(vmem, vmem),
        scratch_shapes=[
            pltpu.SMEM((N_COL,), jnp.int32), pltpu.SMEM((GAPS,), jnp.int32), pltpu.SMEM((GAPS,), jnp.int32),
            pltpu.VMEM((CHUNKS, CHUNK, WINDOWS, FILE_MOST), jnp.bfloat16),
            pltpu.VMEM((CHUNKS, 2 * BINS, TABLE_LANES), jnp.bfloat16),
            pltpu.VMEM((WINDOWS, 4, 64, LANES), jnp.float32),
            pltpu.VMEM((2 * N_ROW, 64, LANES), jnp.float32),
            pltpu.VMEM((8, 64, LANES), jnp.bfloat16),
            pltpu.VMEM((8, 64, LANES), jnp.bfloat16),
            pltpu.VMEM((64, LANES), jnp.bfloat16),
            pltpu.VMEM((2, 4, 2, 64, LANES), jnp.bfloat16),
            pltpu.VMEM((2, FEATURES, LANES), jnp.bfloat16),
            dma((3,)), dma((CHUNKS,)), dma((CHUNKS,)),
            dma((4 * WINDOWS,)), dma((2 * N_ROW,)),
            dma((7,)), dma((8,)),
            dma((8,)), dma((8,)),
            dma((N_ROW,)), dma((N_ROW,)),
            dma((4 // HAND_ON,)), dma((4 // HAND_ON,)),
        ],
        compiler_params=pltpu.CompilerParams(collective_id=0, has_side_effects=True, vmem_limit_bytes=EXCHANGE_VMEM),
        name="exchange",
    )(*[pltpu.with_memory_space_constraint(v, pltpu.HBM) for v in (file_lengths, gap_starts, gap_lengths, jnp.transpose(traces, (2, 1, 0)), table)])
    return pl.pallas_call(
        cross_kernel,
        out_shape=jax.ShapeDtypeStruct((BINS, 2, FILE_MOST, 2 * LANES), jnp.bfloat16),
        in_specs=[vmem, vmem],
        out_specs=anywhere,
        scratch_shapes=[
            pltpu.VMEM((BINS, 2, FILE_MOST, 2 * LANES), jnp.bfloat16),
            dma((BINS, 2)),
        ],
        compiler_params=pltpu.CompilerParams(vmem_limit_bytes=CROSS_VMEM),
        name="cross",
    )(left, right)


def solution(mesh):
    in_specs = (P("col", None, "row"), P(), P(), P())
    out_specs = P(None, None, "row", "col")
    return jax.shard_map(local, mesh=mesh, in_specs=in_specs, out_specs=out_specs, check_vma=False)
```
